256 devices in a mesh: ctx: 16 (over x_lo, z), head: 8 (over y, core), dp: 2 (over x_hi).
Axes of the slice: x: 4 (x_hi: 2, x_lo: 2; x = x_hi * 2 + x_lo), y: 4, z: 8, core: 2. Of those that a mesh axis runs over, the one named last changes fastest.
Arguments:
- inputs: bfloat16 [2, 16384, 4096], P('dp', 'ctx', 'head'), may hold values from -6 to 6
- q_base: bfloat16 [2, 16384, 4096], P('dp', 'ctx', 'head'), may hold values from -20 to 20
- k_base: bfloat16 [2, 16384, 4096], P('dp', 'ctx', 'head'), may hold values from -20 to 20
- v_base: bfloat16 [2, 16384, 4096], P('dp', 'ctx', 'head'), may hold values from -6 to 6
- d_out: bfloat16 [2, 16384, 4096], P('dp', 'ctx', 'head'), may hold values from -0.1796875 to 0.1796875
- d_ctx_base: bfloat16 [2, 16384, 4096], P('dp', 'ctx', 'head'), may hold values from -0.1796875 to 0.1796875
- flags: int32 [32], P('head'), may hold values from 0 to 1, as said below
- query_down_factor: bfloat16 [16, 4096], P(None, 'head'), may hold values from -0.09375 to 0.09375
- up_q: bfloat16 [16, 4096], P(None, 'head'), may hold values from -0.29882812 to 0.29882812
- key_down_factor: bfloat16 [16, 4096], P(None, 'head'), may hold values from -0.09375 to 0.09375
- up_k: bfloat16 [16, 4096], P(None, 'head'), may hold values from -0.29882812 to 0.29882812
- value_down_factor: bfloat16 [16, 4096], P(None, 'head'), may hold values from -0.09375 to 0.09375
- up_v: bfloat16 [16, 4096], P(None, 'head'), may hold values from -0.29882812 to 0.29882812
- down_o: bfloat16 [16, 4096], P(None, 'head'), may hold values from -0.09375 to 0.09375
- output_up_factor: bfloat16 [16, 4096], P(None, 'head'), may hold values from -0.29882812 to 0.29882812
Outputs:
- query_down_gradient: float32 [16, 4096], P(None, 'head')
- query_up_gradient: float32 [16, 4096], P(None, 'head')
- key_down_gradient: float32 [16, 4096], P(None, 'head')
- key_up_gradient: float32 [16, 4096], P(None, 'head')
- value_down_gradient: float32 [16, 4096], P(None, 'head')
- value_up_gradient: float32 [16, 4096], P(None, 'head')
- output_down_gradient: float32 [16, 4096], P(None, 'head')
- output_up_gradient: float32 [16, 4096], P(None, 'head')
The draws below stay inside these ranges and needn't reach their ends.
Inputs may be any that keep to these rules, and one draw needn't show every extreme that they name: `flags`: in every aligned block of 4 heads exactly half are 1.
All inputs are finite; a program needn't handle non-finite values.
Results may differ from the reference program's by a relative error of at most 0.012.
The reference program's roundings to bfloat16 on the way (of `probs_low`, `context` and `grad_scores`) count: a program that leaves them out, or rounds other values in their place, can miss the bound.
Values may be sent and summed in bfloat16 or wider, within the bound.
A program may use at most 128 MiB of HBM per device.

```python
import math
import jax
import jax.numpy as jnp
from jax import lax

D = 4096
HEADS = 32
HD = 128
R = 16
GROUP = 1024
SHIFT = 512
HEADS_DEV = 4
LENGTH = 16384
SEQS = 2


def draw_q_base(key, part):
    key = jax.random.fold_in(key, 1)
    frozen_output = jnp.clip(jax.random.normal(key, (SEQS, LENGTH, D), jnp.float32), -4.0, 4.0)
    return frozen_output.astype(jnp.bfloat16)


def draw_k_base(key, part):
    key = jax.random.fold_in(key, 2)
    frozen_output = jnp.clip(jax.random.normal(key, (SEQS, LENGTH, D), jnp.float32), -4.0, 4.0)
    return frozen_output.astype(jnp.bfloat16)


def draw_flags(key, part):
    key = jax.random.fold_in(key, 3)
    blocks = HEADS // HEADS_DEV
    subkeys = jax.random.split(key, blocks)
    orders = jax.vmap(lambda subkey: jax.random.permutation(subkey, HEADS_DEV))(subkeys)
    return (orders < HEADS_DEV // 2).astype(jnp.int32).reshape(HEADS)


def levels(key, shape, cuts, least, high):
    level = 1.0
    for axis_at, shards_of in cuts:
        heights = jax.random.uniform(jax.random.fold_in(jax.random.fold_in(key, 6), axis_at), (shards_of,), jnp.float32, least / len(cuts), high / len(cuts))
        level = level * jnp.repeat(jnp.exp(heights), shape[axis_at] // shards_of).reshape((-1,) + (1,) * (len(shape) - 1 - axis_at))
    return level


def gaussian(stream_key, shape, deviation, most, pieces=(), held_as=jnp.bfloat16):
    result = jax.random.normal(stream_key, shape, jnp.float32) * deviation
    if len(pieces) > 0:
        result = levels(stream_key, shape, pieces, -0.22, 0.18) * result
    return jnp.clip(result, min=-most, max=most).astype(held_as)


def setup_inputs(seed: int = 0) -> dict:
    splits = jax.random.split(jax.random.key(seed), 16)
    return {
        "inputs": gaussian(splits[0], (SEQS, LENGTH, D), 1.0, 6.0, ((0, 2), (1, 16), (2, 8))),
        "q_base": draw_q_base(jax.random.fold_in(splits[15], 71), 0),
        "k_base": draw_k_base(jax.random.fold_in(splits[15], 71), 0),
        "v_base": gaussian(splits[3], (SEQS, LENGTH, D), 1.0, 6.0, ((0, 2), (1, 16), (2, 8))),
        "d_out": gaussian(splits[4], (SEQS, LENGTH, D), 0.03, 0.1796875, ((0, 2), (1, 16), (2, 8))),
        "d_ctx_base": gaussian(splits[5], (SEQS, LENGTH, D), 0.03, 0.1796875, ((0, 2), (1, 16), (2, 8))),
        "flags": draw_flags(jax.random.fold_in(splits[15], 71), 0),
        "query_down_factor": gaussian(splits[7], (R, D), D ** -0.5, 0.09375, ((1, 8),)),
        "up_q": gaussian(splits[8], (R, D), 0.05, 0.29882812, ((1, 8),)),
        "key_down_factor": gaussian(splits[9], (R, D), D ** -0.5, 0.09375, ((1, 8),)),
        "up_k": gaussian(splits[10], (R, D), 0.05, 0.29882812, ((1, 8),)),
        "value_down_factor": gaussian(splits[11], (R, D), D ** -0.5, 0.09375, ((1, 8),)),
        "up_v": gaussian(splits[12], (R, D), 0.05, 0.29882812, ((1, 8),)),
        "down_o": gaussian(splits[13], (R, D), D ** -0.5, 0.09375, ((1, 8),)),
        "output_up_factor": gaussian(splits[14], (R, D), 0.05, 0.29882812, ((1, 8),)),
    }


adapter_scale = 2.0

def group_reference(query, keys, values, upstream):
    scale = 1.0 / math.sqrt(HD)
    query_f = query.astype(jnp.float32)
    keys_f = keys.astype(jnp.float32)
    values_f = values.astype(jnp.float32)
    upstream_f = upstream.astype(jnp.float32)
    scores = jnp.einsum('gqd,gkd->gqk', query_f, keys_f) * scale
    causal = lax.broadcasted_iota(jnp.int32, (GROUP, GROUP), 0) >= lax.broadcasted_iota(jnp.int32, (GROUP, GROUP), 1)
    scores = jnp.where(causal, scores, -jnp.inf)
    peak = lax.optimization_barrier(jnp.max(scores, axis=-1, keepdims=True))
    weights = jnp.exp(scores - peak)
    probs = weights / lax.optimization_barrier(jnp.sum(weights, axis=-1, keepdims=True))
    probs_low = probs.astype(jnp.bfloat16).astype(jnp.float32)
    context = jnp.einsum('gqk,gkd->gqd', probs_low, values_f).astype(jnp.bfloat16)
    grad_probs = jnp.einsum('gqd,gkd->gqk', upstream_f, values_f)
    center = lax.optimization_barrier(jnp.sum(probs * grad_probs, axis=-1, keepdims=True))
    grad_scores = (probs * (grad_probs - center) * scale).astype(jnp.bfloat16).astype(jnp.float32)
    grad_query = jnp.einsum('gqk,gkd->gqd', grad_scores, keys_f)
    grad_keys = jnp.einsum('gqk,gqd->gkd', grad_scores, query_f)
    grad_values = jnp.einsum('gqk,gqd->gkd', probs_low, upstream_f)
    return (context, grad_query, grad_keys, grad_values)

def reference(inputs, q_base, k_base, v_base, d_out, d_ctx_base, flags, query_down_factor, up_q, key_down_factor, up_k, value_down_factor, up_v, down_o, output_up_factor):
    highest_precision = lax.Precision.HIGHEST
    feature_rows = inputs.astype(jnp.float32)
    output_gradient = d_out.astype(jnp.float32)
    query_latent = jnp.einsum('kbc,xc->kbx', feature_rows, query_down_factor.astype(jnp.float32))
    key_latent = jnp.einsum('kbc,xc->kbx', feature_rows, key_down_factor.astype(jnp.float32))
    value_latent = jnp.einsum('kbc,xc->kbx', feature_rows, value_down_factor.astype(jnp.float32))
    combined_gradient = jnp.einsum('kbc,xc->kbx', output_gradient, output_up_factor.astype(jnp.float32))

    def adapted(frozen_output, latent_rows, upper_factor):
        adapter_extra = jnp.einsum('slr,rc->slc', latent_rows, upper_factor.astype(jnp.float32), precision=highest_precision)
        return (frozen_output.astype(jnp.float32) + adapter_scale * adapter_extra).astype(jnp.bfloat16)
    query = adapted(q_base, query_latent, up_q)
    keys = adapted(k_base, key_latent, up_k)
    values = adapted(v_base, value_latent, up_v)
    upstream = adapted(d_ctx_base, combined_gradient, down_o)

    def one_head(index):
        flag = flags[index]
        start = (index * HD).astype(jnp.int32)

        def pick(array):
            piece = lax.dynamic_slice_in_dim(array, start, HD, 2)
            piece = jnp.where(flag > 0, jnp.roll(piece, -SHIFT, axis=1), piece)
            return piece.reshape(SEQS * LENGTH // GROUP, GROUP, HD)
        results = group_reference(pick(query), pick(keys), pick(values), pick(upstream))
        outputs = []
        for item in results:
            item = item.reshape(SEQS, LENGTH, HD)
            outputs.append(jnp.where(flag > 0, jnp.roll(item, SHIFT, axis=1), item))
        return tuple(outputs)
    context, grad_query, grad_keys, grad_values = lax.map(one_head, jnp.arange(HEADS, dtype=jnp.int32))

    def merge_heads(array):
        return jnp.moveaxis(array, 0, 2).reshape(SEQS, LENGTH, D)
    context = merge_heads(context)
    grad_query = merge_heads(grad_query)
    grad_keys = merge_heads(grad_keys)
    grad_values = merge_heads(grad_values)
    context_f = context.astype(jnp.float32)
    g_q = jnp.einsum('slc,rc->slr', grad_query, up_q.astype(jnp.float32), precision=highest_precision)
    g_k = jnp.einsum('slc,rc->slr', grad_keys, up_k.astype(jnp.float32), precision=highest_precision)
    g_v = jnp.einsum('slc,rc->slr', grad_values, up_v.astype(jnp.float32), precision=highest_precision)
    lat_o = jnp.einsum('slc,rc->slr', context_f, down_o.astype(jnp.float32))

    def outer(left_operand, right_operand):
        return adapter_scale * jnp.einsum('fde,fdm->em', left_operand, right_operand, precision=highest_precision)
    return (outer(g_q, feature_rows), outer(query_latent, grad_query), outer(g_k, feature_rows), outer(key_latent, grad_keys), outer(g_v, feature_rows), outer(value_latent, grad_values), outer(combined_gradient, context_f), outer(lat_o, output_gradient))
```

```python
import functools
import math

import jax
import jax.numpy as jnp
from jax import lax
from jax.experimental import pallas as pl
from jax.experimental.pallas import tpu as pltpu
from jax.sharding import PartitionSpec as P

HD = 128
ROWS = 1024
HALF = 512
CHUNK = 256
RANK = 16
WIDTH = 512
NY, NZ, NX = 4, 8, 4
SCALE = 1.0 / math.sqrt(HD)
EXP_SCALE = SCALE * math.log2(math.e)
MESH = pl.DeviceIdType.MESH
F32 = jnp.float32
BF16 = jnp.bfloat16
NN = (((1,), (0,)), ((), ()))
NT = (((1,), (1,)), ((), ()))


def dot(a, b, dims=NN):
    return lax.dot_general(a, b, dims, preferred_element_type=F32)


def place(block):
    return (block // 2) % 2 * 4 + block % 2 + 2 * (block // 4)


def split_rows(wide, kinds):
    rows = []
    for t in range(kinds):
        part = wide[RANK * t : RANK * (t + 1)]
        high = part.astype(BF16).astype(F32)
        rows += [high, part - high]
    return jnp.concatenate(rows, axis=0)


def fold(pair):
    return pair[:RANK] + pair[RANK:]


def chunk_scores(keys, values, keys_t, values_t, query, upstream):
    length = keys.shape[0]
    scores = dot(keys, query, NT)
    own = scores[length - CHUNK :]
    causal = lax.broadcasted_iota(jnp.int32, own.shape, 0) <= lax.broadcasted_iota(
        jnp.int32, own.shape, 1
    )
    own = jnp.where(causal, own, -jnp.inf)
    scores = own if length == CHUNK else jnp.concatenate([scores[: length - CHUNK], own], axis=0)
    peak = jnp.max(scores, axis=0, keepdims=True)
    weights = jnp.exp2((scores - peak) * EXP_SCALE)
    probs = weights * (1.0 / jnp.sum(weights, axis=0, keepdims=True))
    grad_probs = dot(values, upstream, NT)
    center = jnp.sum(probs * grad_probs, axis=0, keepdims=True)
    grad_scores = (probs * (grad_probs - center) * SCALE).astype(BF16)
    probs_low = probs.astype(BF16)
    context_t = dot(values_t, probs_low)
    grad_query_t = dot(keys_t, grad_scores)
    return probs_low, grad_scores, context_t.astype(BF16), grad_query_t.astype(BF16)


def kernel(
    x_hbm, q_hbm, k_hbm, v_hbm, do_hbm, dc_hbm, flags,
    down_q, up_q, down_k, up_k, down_v, up_v, down_o, up_o,
    out_ref,
    xb, qb, kb, vb, dob, dcb,
    kv_stage, kv_in,
    part, sib_in, acc, y_in, total,
    lat_prev, up_pad, fac, prev_up, lat_low, prev_low, prev_cols,
    qa, ka, va, ua, kt, vt,
    grads, back, back_in, up_sum,
    cut, x_in, x_sum, z_in, z_all, x_all,
    load_sem, kv_send, kv_recv, lp_send, lp_recv, back_send, back_recv,
    sib_send, sib_recv, y1_send, y1_recv, y2_send, y2_recv, fw_send, fw_recv,
    x1_send, x1_recv, z1_send, z1_recv, z2_send, z2_recv, x2_send, x2_recv,
):
    ctx, head, dp = lax.axis_index("ctx"), lax.axis_index("head"), lax.axis_index("dp")
    y, core = head // 2, head % 2
    x_lo, z = ctx // NZ, ctx % NZ
    x = dp * 2 + x_lo
    sibling = {"head": y * 2 + (1 - core)}
    after = lax.rem(ctx + 1, 2 * NZ)
    before = lax.rem(ctx + 2 * NZ - 1, 2 * NZ)

    def y_peer(d):
        return {"head": lax.rem(y + d, NY) * 2 + core}

    def z_peer(d):
        return {"ctx": x_lo * NZ + lax.rem(z + d, NZ)}

    def x_peer(d):
        other = lax.rem(x + d, NX)
        return {"ctx": (other % 2) * NZ + z, "dp": other // 2}

    loads = []
    pairs = [(x_hbm, xb), (do_hbm, dob)]
    for source, target in ((k_hbm, kb), (v_hbm, vb), (q_hbm, qb), (dc_hbm, dcb)):
        pairs += [(source.at[:, pl.ds(HD * h, HD)], target.at[h]) for h in range(4)]
    for i, (source, target) in enumerate(pairs):
        copy = pltpu.make_async_copy(source, target, load_sem.at[i])
        copy.start()
        loads.append(copy)

    barrier = pltpu.get_barrier_semaphore()
    peers = [sibling]
    peers += [y_peer(d) for d in range(1, NY)]
    peers += [z_peer(d) for d in range(1, NZ)]
    peers += [x_peer(d) for d in range(1, NX)]
    for near in (after, before):
        peers += [{"ctx": near}, {"ctx": near, "head": y * 2 + (1 - core)}]
    for peer in peers:
        pl.semaphore_signal(barrier, inc=1, device_id=peer, device_id_type=MESH)

    sends = []

    def remote(source, target, send_sem, recv_sem, peer):
        return pltpu.make_async_remote_copy(
            src_ref=source, dst_ref=target, send_sem=send_sem, recv_sem=recv_sem,
            device_id=peer, device_id_type=MESH,
        )

    def send(*args):
        copy = remote(*args)
        copy.start()
        sends.append(copy)

    f0, f1, f2, f3 = (flags[h] for h in range(4))
    head_of = (
        (1 - f0) * (2 - f1),
        3 * f3 + (1 - f3) * (1 + f2),
        f0 * (1 + f1),
        3 * (1 - f3) + f3 * (2 - f2),
    )
    slot_of = (
        2 - 2 * f0,
        f1 * f0 + (1 - f1) * (2 + 1 - f0),
        f2 * (f0 + f1) + (1 - f2) * (4 - f0 - f1),
        f3 + (1 - f3) * 3,
    )

    up_pad[...] = jnp.zeros_like(up_pad)
    for t, factor in enumerate((up_q, up_k, up_v, down_o)):
        for copy_at in (0, RANK):
            up_pad[32 * t + copy_at : 32 * t + copy_at + RANK, WIDTH * t : WIDTH * (t + 1)] = factor[...]
        for h in range(4):
            fac[t, h] = factor[:, HD * h : HD * (h + 1)]
    for t in range(2):
        for h in range(4):
            at = WIDTH * (1 + t) + HD * h
            prev_up[t, h] = up_pad[32:96, at : at + HD]
    grads[...] = jnp.zeros_like(grads)
    back[...] = jnp.zeros_like(back)
    up_sum[...] = jnp.zeros_like(up_sum)

    loads[0].wait()
    first = jnp.concatenate([down_q[...], down_k[...], down_v[...]], axis=0)
    lat_part = dot(first, xb[...], NT)
    loads[1].wait()
    mix_part = dot(up_o[...], dob[...], NT)
    for b in range(8):
        part[0, place(b), :48] = lat_part[:, HD * b : HD * (b + 1)]
        part[0, place(b), 48:] = mix_part[:, HD * b : HD * (b + 1)]

    pl.semaphore_wait(barrier, len(peers))

    def sum_heads(p, late=None):
        mine = core * 4
        other = (1 - core) * 4
        send(part.at[p, pl.ds(other, 4)], sib_in.at[p], sib_send.at[p], sib_recv.at[p], sibling)
        yield
        remote(part.at[p, pl.ds(other, 4)], sib_in.at[p], sib_send.at[p], sib_recv.at[p], sibling).wait_recv()
        for i in range(4):
            acc[p, i] = part[p, mine + i] + sib_in[p, i]
        if late is not None:
            late()
        for d in range(1, NY):
            send(acc.at[p, lax.rem(y + d, NY)], y_in.at[p, d - 1], y1_send.at[p, d - 1], y1_recv.at[p, d - 1], y_peer(d))
        yield
        for d in range(1, NY):
            remote(acc.at[p, 0], y_in.at[p, d - 1], y1_send.at[p, d - 1], y1_recv.at[p, d - 1], y_peer(d)).wait_recv()
        own = total.at[p, mine + y]
        own[...] = acc[p, y] + y_in[p, 0] + y_in[p, 1] + y_in[p, 2]
        for d in range(1, NY):
            send(own, own, y2_send.at[p, d - 1], y2_recv.at[p, d - 1], y_peer(d))
        send(own, own, fw_send.at[p, 0], fw_recv.at[p, 0], sibling)
        yield
        for d in range(1, NY):
            came = total.at[p, mine + lax.rem(y + NY - d, NY)]
            remote(came, came, y2_send.at[p, d - 1], y2_recv.at[p, d - 1], y_peer(d)).wait_recv()
            send(came, came, fw_send.at[p, d], fw_recv.at[p, d], sibling)
        yield
        for d in range(NY):
            came = total.at[p, other + lax.rem(y + NY - d, NY)]
            remote(came, came, fw_send.at[p, d], fw_recv.at[p, d], sibling).wait_recv()
        yield

    def sum_tokens(e):
        for d in range(1, NX):
            send(cut.at[e, lax.rem(x + d, NX)], x_in.at[e, d - 1], x1_send.at[e, d - 1], x1_recv.at[e, d - 1], x_peer(d))
        yield
        for d in range(1, NX):
            remote(cut.at[e, 0], x_in.at[e, d - 1], x1_send.at[e, d - 1], x1_recv.at[e, d - 1], x_peer(d)).wait_recv()
        x_sum[e] = cut[e, x] + x_in[e, 0] + x_in[e, 1] + x_in[e, 2]
        for d in range(1, NZ):
            send(x_sum.at[e, lax.rem(z + d, NZ)], z_in.at[e, d - 1], z1_send.at[e, d - 1], z1_recv.at[e, d - 1], z_peer(d))
        yield
        for d in range(1, NZ):
            remote(x_sum.at[e, 0], z_in.at[e, d - 1], z1_send.at[e, d - 1], z1_recv.at[e, d - 1], z_peer(d)).wait_recv()
        own = z_all.at[e, z]
        summed = x_sum[e, z]
        for d in range(1, NZ):
            summed = summed + z_in[e, d - 1]
        own[...] = summed
        for d in range(1, NZ):
            send(own, own, z2_send.at[e, d - 1], z2_recv.at[e, d - 1], z_peer(d))
        yield
        for d in range(1, NZ):
            came = z_all.at[e, lax.rem(z + NZ - d, NZ)]
            remote(came, came, z2_send.at[e, d - 1], z2_recv.at[e, d - 1], z_peer(d)).wait_recv()
        for d in range(1, NX):
            send(z_all.at[e], x_all.at[e, x], x2_send.at[e, d - 1], x2_recv.at[e, d - 1], x_peer(d))
        x_all[e, x] = z_all[e]
        yield
        for d in range(1, NX):
            came = x_all.at[e, lax.rem(x + NX - d, NX)]
            remote(z_all.at[e], came, x2_send.at[e, d - 1], x2_recv.at[e, d - 1], x_peer(d)).wait_recv()
        for c in range(4):
            for r in range(8):
                out_ref[e, 8 * r : 8 * r + 8, HD * c : HD * (c + 1)] = x_all[e, c, r]
        yield

    latents = sum_heads(0)
    next(latents)

    for copy in loads[2:10]:
        copy.wait()
    for s in range(2):
        for i, base in enumerate((kb, vb)):
            kv_stage[s, i] = base[head_of[s], HALF:, :]
        send(kv_stage.at[s], kv_in.at[s], kv_send.at[s], kv_recv.at[s], {"ctx": after})

    for _ in range(4):
        next(latents)

    for c in range(2):
        send(
            total.at[0, pl.ds(4 * c + 2, 2), pl.ds(RANK, 2 * RANK)], lat_prev.at[pl.ds(2 * c, 2)],
            lp_send.at[c], lp_recv.at[c], {"ctx": after},
        )
    for copy in loads[10:]:
        copy.wait()

    def adapt(b, carry):
        rows = pl.ds(pl.multiple_of(b * HD, HD), HD)
        both = split_rows(2.0 * total[0, place(b)], 4)
        lat_low[:, rows] = both.astype(BF16)
        extra = dot(both.T.astype(BF16), up_pad[...])
        for t, (base, full, turned) in enumerate(
            ((qb, qa, None), (kb, ka, kt), (vb, va, vt), (dcb, ua, None))
        ):
            for h in range(4):
                at = WIDTH * t + HD * h
                low = (base[h, rows, :].astype(F32) + extra[:, at : at + HD]).astype(BF16)
                full[h, rows, :] = low
                if turned is not None:
                    turned[h, :, rows] = low.T
        return carry

    lax.fori_loop(0, 8, adapt, 0)

    for c in range(2):
        remote(
            total.at[0, pl.ds(4 * c + 2, 2), pl.ds(RANK, 2 * RANK)], lat_prev.at[pl.ds(2 * c, 2)],
            lp_send.at[c], lp_recv.at[c], {"ctx": after},
        ).wait_recv()
    for b in range(4):
        both = split_rows(2.0 * lat_prev[b], 2)
        prev_low[:, HD * b : HD * (b + 1)] = both.astype(BF16)
        prev_cols[HD * b : HD * (b + 1), :] = both.T.astype(BF16)

    def attend(slot, h, first_at, off):
        last_at = HALF - first_at
        uq, uk, uv, od = (fac[t, h] for t in range(4))
        off_k, off_v, off_kt, off_vt = off if off is not None else (
            ka[h, :HALF, :], va[h, :HALF, :], kt[h, :, :HALF], vt[h, :, :HALF],
        )
        sums = [0.0, 0.0, 0.0, 0.0]

        def keys_done(t, factor, grad, lat, put):
            low = grad.astype(BF16)
            put(t, dot(factor, low, NT))
            sums[t] = sums[t] + fold(dot(lat, low))

        def queries_done(t, factor, grad_t, lat, put):
            put(t, dot(factor, grad_t))
            sums[t] = sums[t] + fold(dot(lat, grad_t, NT))

        def lat_of(t, at):
            return lat_low[32 * t : 32 * t + 32, at : at + HALF]

        def put_at(at):
            def put(t, value):
                grads[RANK * t : RANK * (t + 1), at : at + HALF] += value
            return put

        def put_back(t, value):
            for b in range(4):
                back[b // 2, b % 2, RANK * (t - 1) : RANK * t] += value[:, HD * b : HD * (b + 1)]

        for at, with_off in ((first_at, False), (last_at, True)):
            own = slice(at, at + HALF)
            keys, values = ka[h, own, :], va[h, own, :]
            keys_t, values_t = kt[h, :, own], vt[h, :, own]
            query, upstream = qa[h, own, :], ua[h, own, :]
            ahead = 0
            if with_off:
                ahead = HALF
                keys = jnp.concatenate([off_k, keys], axis=0)
                values = jnp.concatenate([off_v, values], axis=0)
                keys_t = jnp.concatenate([off_kt, keys_t], axis=1)
                values_t = jnp.concatenate([off_vt, values_t], axis=1)
            results = []
            for c in range(2):
                length = ahead + CHUNK * (c + 1)
                here = slice(CHUNK * c, CHUNK * (c + 1))
                results.append(
                    chunk_scores(
                        keys[:length], values[:length], keys_t[:, :length], values_t[:, :length],
                        query[here], upstream[here],
                    )
                )
            short = ahead + CHUNK
            (p0, s0, c0, q0), (p1, s1, c1, q1) = results

            def over_queries(early, late, rows):
                return jnp.concatenate(
                    [
                        dot(early, rows[:CHUNK]) + dot(late[:short], rows[CHUNK:]),
                        dot(late[short:], rows[CHUNK:]),
                    ],
                    axis=0,
                )

            grad_keys = over_queries(s0, s1, query)
            grad_values = over_queries(p0, p1, upstream)
            queries_done(0, uq, jnp.concatenate([q0, q1], axis=1), lat_of(0, at), put_at(at))
            queries_done(3, od, jnp.concatenate([c0, c1], axis=1), lat_of(3, at), put_at(at))
            for t, factor, grad in ((1, uk, grad_keys), (2, uv, grad_values)):
                keys_done(t, factor, grad[ahead:], lat_of(t, at), put_at(at))
                if with_off and off is None:
                    keys_done(t, factor, grad[:ahead], lat_of(t, 0), put_at(0))
                elif with_off:
                    keys_done(t, factor, grad[:ahead], prev_low[32 * t - 32 : 32 * t, :], put_back)
        for t in range(4):
            up_sum[slot, RANK * t : RANK * (t + 1)] = sums[t]

    def back_copy(c):
        return remote(
            back.at[c], back_in.at[core], back_send.at[c], back_recv.at[core],
            {"ctx": before, "head": y * 2 + c},
        )

    def both_kinds(i, carry):
        h = head_of[0] + i * (head_of[1] - head_of[0])
        still = head_of[2] + i * (head_of[3] - head_of[2])
        remote(kv_stage.at[i], kv_in.at[i], kv_send.at[i], kv_recv.at[i], {"ctx": after}).wait_recv()
        off_k = (kv_in[i, 0].astype(F32) + dot(prev_cols[...], prev_up[0, h])).astype(BF16)
        off_v = (kv_in[i, 1].astype(F32) + dot(prev_cols[...], prev_up[1, h])).astype(BF16)
        attend(i, h, HALF, (off_k, off_v, off_k.T, off_v.T))

        @pl.when(i == 1)
        def _():
            for c in range(2):
                back_copy(c).start()

        attend(2 + i, still, 0, None)
        return carry

    lax.fori_loop(0, 2, both_kinds, 0)

    for b in range(8):
        part[1, place(b)] = grads[:, HD * b : HD * (b + 1)]

    def add_back():
        for c in range(2):
            remote(back.at[c], back_in.at[c], back_send.at[c], back_recv.at[c], sibling).wait_recv()
        for i in range(2):
            acc[1, 2 + i, RANK : 3 * RANK] += back_in[0, i] + back_in[1, i]

    shares = sum_heads(1, add_back)
    next(shares)
    for h in range(4):
        piece = up_sum[jnp.minimum(slot_of[h], 3)]
        for r in range(8):
            cut[0, h, r] = piece[8 * r : 8 * r + 8]
    ups = sum_tokens(0)
    next(ups)
    next(shares)
    next(ups)
    next(shares)
    next(ups)
    next(shares)
    next(shares)

    wide = []
    for b in range(8):
        wide.append(split_rows(2.0 * total[1, place(b)], 4).astype(BF16))
    wide = jnp.concatenate(wide, axis=1)
    down = dot(wide[:96], xb[...])
    last = fold(dot(wide[96:], dob[...]))
    down = jnp.concatenate([fold(down[32 * t : 32 * t + 32]) for t in range(3)] + [last], axis=0)
    for c in range(4):
        for r in range(8):
            cut[1, c, r] = down[8 * r : 8 * r + 8, HD * c : HD * (c + 1)]
    downs = sum_tokens(1)
    next(downs)
    next(ups)
    next(downs)
    next(downs)
    next(ups)
    next(downs)
    next(downs)
    for copy in sends:
        copy.wait_send()
    for c in range(2):
        back_copy(c).wait_send()


def on_device(
    inputs, q_base, k_base, v_base, d_out, d_ctx_base, flags,
    query_down_factor, up_q, key_down_factor, up_k, value_down_factor, up_v, down_o, output_up_factor,
):
    anywhere = pl.BlockSpec(memory_space=pl.ANY)
    vmem = pl.BlockSpec(memory_space=pltpu.VMEM)
    smem = pl.BlockSpec(memory_space=pltpu.SMEM)
    dma = pltpu.SemaphoreType.DMA
    v = pltpu.VMEM
    out = pl.pallas_call(
        kernel,
        out_shape=jax.ShapeDtypeStruct((2, 64, WIDTH), F32),
        in_specs=[anywhere] * 6 + [smem] + [vmem] * 8,
        out_specs=vmem,
        scratch_shapes=[
            *[v((ROWS, WIDTH), BF16) for _ in range(1)], *[v((4, ROWS, HD), BF16) for _ in range(3)],
            v((ROWS, WIDTH), BF16), v((4, ROWS, HD), BF16),
            v((2, 2, HALF, HD), BF16), v((2, 2, HALF, HD), BF16),
            v((2, 8, 64, HD), F32), v((2, 4, 64, HD), F32), v((2, 4, 64, HD), F32),
            v((2, 3, 64, HD), F32), v((2, 8, 64, HD), F32),
            v((4, 32, HD), F32), v((128, 4 * WIDTH), BF16), v((4, 4, RANK, HD), BF16),
            v((2, 4, 64, HD), BF16), v((128, ROWS), BF16),
            v((64, HALF), BF16), v((HALF, 64), BF16),
            *[v((4, ROWS, HD), BF16) for _ in range(4)],
            *[v((4, HD, ROWS), BF16) for _ in range(2)],
            v((64, ROWS), F32), v((2, 2, 32, HD), F32), v((2, 2, 32, HD), F32), v((4, 64, HD), F32),
            v((2, 4, 8, 8, HD), F32), v((2, 3, 8, 8, HD), F32), v((2, 8, 8, HD), F32),
            v((2, 7, 8, HD), F32), v((2, 8, 8, HD), F32), v((2, 4, 8, 8, HD), F32),
            dma((18,)), dma((2,)), dma((2,)), dma((2,)), dma((2,)), dma((2,)), dma((2,)),
            dma((2,)), dma((2,)), dma((2, 3)), dma((2, 3)), dma((2, 3)), dma((2, 3)), dma((2, 4)), dma((2, 4)),
            dma((2, 3)), dma((2, 3)), dma((2, 7)), dma((2, 7)), dma((2, 7)), dma((2, 7)), dma((2, 3)), dma((2, 3)),
        ],
        compiler_params=pltpu.CompilerParams(
            collective_id=0, has_side_effects=True, vmem_limit_bytes=56 * 1024 * 1024
        ),
    )(
        inputs[0], q_base[0], k_base[0], v_base[0], d_out[0], d_ctx_base[0], flags,
        query_down_factor, up_q, key_down_factor, up_k, value_down_factor, up_v, down_o, output_up_factor,
    )
    result = []
    for t in range(4):
        rows = slice(RANK * t, RANK * (t + 1))
        result += [out[1, rows], out[0, rows]]
    return (result[0], result[1], result[2], result[3], result[4], result[5], result[7], result[6])


def solution(mesh):
    tokens = P("dp", "ctx", "head")
    factor = P(None, "head")
    return jax.shard_map(
        on_device,
        mesh=mesh,
        in_specs=(tokens,) * 6 + (P("head"),) + (factor,) * 8,
        out_specs=(factor,) * 8,
        check_vma=False,
    )
```

```python
import functools
import math

import jax
import jax.numpy as jnp
from jax import lax
from jax.experimental import pallas as pl
from jax.experimental.pallas import tpu as pltpu
from jax.sharding import PartitionSpec as P

HD = 128
ROWS = 1024
HALF = 512
CHUNK = 256
RANK = 16
WIDTH = 512
NY, NZ, NX = 4, 8, 4
SCALE = 1.0 / math.sqrt(HD)
EXP_SCALE = SCALE * math.log2(math.e)
MESH = pl.DeviceIdType.MESH
F32 = jnp.float32
BF16 = jnp.bfloat16
NN = (((1,), (0,)), ((), ()))
NT = (((1,), (1,)), ((), ()))


def dot(a, b, dims=NN):
    return lax.dot_general(a, b, dims, preferred_element_type=F32)


def place(block):
    return (block // 2) % 2 * 4 + block % 2 + 2 * (block // 4)


def split_rows(wide, kinds):
    rows = []
    for t in range(kinds):
        part = wide[RANK * t : RANK * (t + 1)]
        high = part.astype(BF16).astype(F32)
        rows += [high, part - high]
    return jnp.concatenate(rows, axis=0)


def fold(pair):
    return pair[:RANK] + pair[RANK:]


def chunk_scores(keys, values, keys_t, values_t, query, upstream):
    length = keys.shape[0]
    scores = dot(keys, query, NT)
    own = scores[length - CHUNK :]
    causal = lax.broadcasted_iota(jnp.int32, own.shape, 0) <= lax.broadcasted_iota(
        jnp.int32, own.shape, 1
    )
    own = jnp.where(causal, own, -jnp.inf)
    scores = own if length == CHUNK else jnp.concatenate([scores[: length - CHUNK], own], axis=0)
    peak = jnp.max(scores, axis=0, keepdims=True)
    weights = jnp.exp2((scores - peak) * EXP_SCALE)
    probs = weights * (1.0 / jnp.sum(weights, axis=0, keepdims=True))
    grad_probs = dot(values, upstream, NT)
    center = jnp.sum(probs * grad_probs, axis=0, keepdims=True)
    grad_scores = (probs * (grad_probs - center) * SCALE).astype(BF16)
    probs_low = probs.astype(BF16)
    context_t = dot(values_t, probs_low)
    grad_query_t = dot(keys_t, grad_scores)
    return probs_low, grad_scores, context_t.astype(BF16), grad_query_t.astype(BF16)


def kernel(
    x_hbm, q_hbm, k_hbm, v_hbm, do_hbm, dc_hbm, flags,
    down_q_hbm, up_q_hbm, down_k_hbm, up_k_hbm, down_v_hbm, up_v_hbm, down_o_hbm, up_o_hbm,
    out_ref,
    firsts, seconds,
    xb, qb, kb, vb, dob, dcb,
    kv_stage, kv_in,
    part, sib_in, acc, y_in, total,
    lat_prev, up_pad, fac, prev_up, lat_low, prev_low, prev_cols,
    qa, ka, va, ua, kt, vt,
    grads, back, back_in, up_sum,
    cut, x_in, x_sum, z_in, z_all, x_all,
    load_sem, kv_send, kv_recv, lp_send, lp_recv, back_send, back_recv,
    sib_send, sib_recv, y_send, y_recv, fw_send, fw_recv,
    x1_send, x1_recv, z_send, z_recv, x2_send, x2_recv,
):
    ctx, head, dp = lax.axis_index("ctx"), lax.axis_index("head"), lax.axis_index("dp")
    y, core = head // 2, head % 2
    x_lo, z = ctx // NZ, ctx % NZ
    x = dp * 2 + x_lo
    sibling = {"head": y * 2 + (1 - core)}
    after = lax.rem(ctx + 1, 2 * NZ)
    before = lax.rem(ctx + 2 * NZ - 1, 2 * NZ)

    def y_peer(d):
        return {"head": lax.rem(y + d, NY) * 2 + core}

    def z_peer(d):
        return {"ctx": x_lo * NZ + lax.rem(z + d, NZ)}

    def x_peer(d):
        other = lax.rem(x + d, NX)
        return {"ctx": (other % 2) * NZ + z, "dp": other // 2}

    loads = []

    def load(*pairs):
        for source, target in pairs:
            copy = pltpu.make_async_copy(source, target, load_sem.at[len(loads)])
            copy.start()
            loads.append(copy)

    def by_head(source, target):
        return [(source.at[:, pl.ds(HD * h, HD)], target.at[h]) for h in range(4)]

    load(
        (down_q_hbm, firsts.at[0]), (down_k_hbm, firsts.at[1]), (down_v_hbm, firsts.at[2]), (up_o_hbm, firsts.at[3]),
        (x_hbm, xb), (do_hbm, dob),
        (up_q_hbm, seconds.at[0]), (up_k_hbm, seconds.at[1]), (up_v_hbm, seconds.at[2]), (down_o_hbm, seconds.at[3]),
        *by_head(k_hbm, kb), *by_head(v_hbm, vb),
    )

    barrier = pltpu.get_barrier_semaphore()
    peers = [sibling]
    peers += [y_peer(d) for d in range(1, NY)]
    peers += [z_peer(d) for d in range(1, NZ)]
    peers += [x_peer(d) for d in range(1, NX)]
    for near in (after, before):
        peers += [{"ctx": near}, {"ctx": near, "head": y * 2 + (1 - core)}]
    for peer in peers:
        pl.semaphore_signal(barrier, inc=1, device_id=peer, device_id_type=MESH)

    sends = []

    def remote(source, target, send_sem, recv_sem, peer):
        return pltpu.make_async_remote_copy(
            src_ref=source, dst_ref=target, send_sem=send_sem, recv_sem=recv_sem,
            device_id=peer, device_id_type=MESH,
        )

    def send(*args):
        copy = remote(*args)
        copy.start()
        sends.append(copy)

    f0, f1, f2, f3 = (flags[h] for h in range(4))
    head_of = (
        (1 - f0) * (2 - f1),
        3 * f3 + (1 - f3) * (1 + f2),
        f0 * (1 + f1),
        3 * (1 - f3) + f3 * (2 - f2),
    )
    slot_of = (
        2 - 2 * f0,
        f1 * f0 + (1 - f1) * (2 + 1 - f0),
        f2 * (f0 + f1) + (1 - f2) * (4 - f0 - f1),
        f3 + (1 - f3) * 3,
    )

    def own_latents(owner):
        first = firsts[...].reshape(4 * RANK, WIDTH)
        for j in range(2):
            rows = pl.ds(pl.multiple_of(owner * 256 + HALF * j, 256), 256)
            lat_part = dot(first[: 3 * RANK], xb[rows, :], NT)
            mix_part = dot(first[3 * RANK :], dob[rows, :], NT)
            for k in range(2):
                part[0, owner * 4 + 2 * j + k, : 3 * RANK] = lat_part[:, HD * k : HD * (k + 1)]
                part[0, owner * 4 + 2 * j + k, 3 * RANK :] = mix_part[:, HD * k : HD * (k + 1)]

    for copy in loads[:6]:
        copy.wait()
    with jax.named_scope("own_latents"):
        own_latents(1 - core)
    with jax.named_scope("entry_barrier"):
        pl.semaphore_wait(barrier, len(peers))

    mine = core * 4
    other = (1 - core) * 4

    def sum_heads(p, late=None):
        pair = (part.at[p, pl.ds(other, 4)], sib_in.at[p], sib_send.at[p], sib_recv.at[p], sibling)
        send(*pair)
        yield
        remote(*pair).wait_recv()
        extra = [0.0] * 4 if late is None else late()
        for i in range(4):
            acc[p, i] = (part[p, mine + i] + sib_in[p, i] + extra[i]).astype(BF16)
        shares = [(acc.at[p], y_in.at[p, d - 1], y_send.at[p, d - 1], y_recv.at[p, d - 1], y_peer(d)) for d in range(1, NY)]
        for share in shares:
            send(*share)
        yield
        for share in shares:
            remote(*share).wait_recv()
        for i in range(4):
            summed = acc[p, i].astype(F32)
            for d in range(1, NY):
                summed = summed + y_in[p, d - 1, i].astype(F32)
            total[p, mine + i] = summed
        own = total.at[p, pl.ds(mine, 4)]
        send(own, own, fw_send.at[p], fw_recv.at[p], sibling)
        yield
        came = total.at[p, pl.ds(other, 4)]
        remote(came, came, fw_send.at[p], fw_recv.at[p], sibling).wait_recv()
        yield

    def sum_tokens(e):
        for d in range(1, NX):
            send(cut.at[e, lax.rem(x + d, NX)], x_in.at[e, d - 1], x1_send.at[e, d - 1], x1_recv.at[e, d - 1], x_peer(d))
        yield
        summed = cut[e, x].astype(F32)
        for d in range(1, NX):
            remote(cut.at[e, 0], x_in.at[e, d - 1], x1_send.at[e, d - 1], x1_recv.at[e, d - 1], x_peer(d)).wait_recv()
            summed = summed + x_in[e, d - 1].astype(F32)
        x_sum[e] = summed.astype(BF16)
        shares = [(x_sum.at[e], z_in.at[e, d - 1], z_send.at[e, d - 1], z_recv.at[e, d - 1], z_peer(d)) for d in range(1, NZ)]
        for share in shares:
            send(*share)
        yield
        summed = x_sum[e].astype(F32)
        for d, share in enumerate(shares):
            remote(*share).wait_recv()
            summed = summed + z_in[e, d].astype(F32)
        z_all[e] = summed.astype(BF16)
        for d in range(1, NX):
            send(z_all.at[e], x_all.at[e, x], x2_send.at[e, d - 1], x2_recv.at[e, d - 1], x_peer(d))
        x_all[e, x] = z_all[e]
        yield
        for d in range(1, NX):
            came = x_all.at[e, lax.rem(x + NX - d, NX)]
            remote(z_all.at[e], came, x2_send.at[e, d - 1], x2_recv.at[e, d - 1], x_peer(d)).wait_recv()
        for c in range(4):
            out_ref[e, :, HD * c : HD * (c + 1)] = x_all[e, c].astype(F32)
        yield

    latents = sum_heads(0)
    next(latents)
    with jax.named_scope("own_latents"):
        own_latents(core)

    with jax.named_scope("stage_keys"):
        for copy in loads[10:18]:
            copy.wait()
        for s in range(2):
            for i, base in enumerate((kb, vb)):
                kv_stage[s, i] = base[head_of[s], HALF:, :]
            send(kv_stage.at[s], kv_in.at[s], kv_send.at[s], kv_recv.at[s], {"ctx": after})

    load(*by_head(q_hbm, qb), *by_head(dc_hbm, dcb))
    for copy in loads[6:10]:
        copy.wait()
    up_pad[...] = jnp.zeros_like(up_pad)
    for t, factor in enumerate(seconds[t] for t in range(4)):
        for copy_at in (0, RANK):
            up_pad[32 * t + copy_at : 32 * t + copy_at + RANK, WIDTH * t : WIDTH * (t + 1)] = factor
        for h in range(4):
            fac[t, h] = factor[:, HD * h : HD * (h + 1)]
    for t in range(2):
        for h in range(4):
            at = WIDTH * (1 + t) + HD * h
            prev_up[t, h] = up_pad[32:96, at : at + HD]
    grads[...] = jnp.zeros_like(grads)
    back[...] = jnp.zeros_like(back)
    up_sum[...] = jnp.zeros_like(up_sum)

    with jax.named_scope("latent_sum"):
        next(latents)
        next(latents)

    def adapt(i, owner):
        b = owner * 2 + i % 2 + 4 * (i // 2)
        rows = pl.ds(pl.multiple_of(b * HD, HD), HD)
        both = split_rows(2.0 * total[0, owner * 4 + i], 4)
        lat_low[:, rows] = both.astype(BF16)
        extra = dot(both.T.astype(BF16), up_pad[...])
        for t, (base, full, turned) in enumerate(
            ((qb, qa, None), (kb, ka, kt), (vb, va, vt), (dcb, ua, None))
        ):
            for h in range(4):
                at = WIDTH * t + HD * h
                low = (base[h, rows, :].astype(F32) + extra[:, at : at + HD]).astype(BF16)
                full[h, rows, :] = low
                if turned is not None:
                    turned[h, :, rows] = low.T
        return owner

    for copy in loads[18:]:
        copy.wait()
    with jax.named_scope("adapt"):
        lax.fori_loop(0, 4, adapt, core)
    with jax.named_scope("latent_sum"):
        next(latents)
    for c in range(2):
        send(
            total.at[0, pl.ds(4 * c + 2, 2), pl.ds(RANK, 2 * RANK)], lat_prev.at[pl.ds(2 * c, 2)],
            lp_send.at[c], lp_recv.at[c], {"ctx": after},
        )
    with jax.named_scope("adapt"):
        lax.fori_loop(0, 4, adapt, 1 - core)
        for c in range(2):
            remote(
                total.at[0, pl.ds(4 * c + 2, 2), pl.ds(RANK, 2 * RANK)], lat_prev.at[pl.ds(2 * c, 2)],
                lp_send.at[c], lp_recv.at[c], {"ctx": after},
            ).wait_recv()
        for b in range(4):
            both = split_rows(2.0 * lat_prev[b], 2)
            prev_low[:, HD * b : HD * (b + 1)] = both.astype(BF16)
            prev_cols[HD * b : HD * (b + 1), :] = both.T.astype(BF16)

    def attend(slot, h, first_at, off):
        last_at = HALF - first_at
        uq, uk, uv, od = (fac[t, h] for t in range(4))
        off_k, off_v, off_kt, off_vt = off if off is not None else (
            ka[h, :HALF, :], va[h, :HALF, :], kt[h, :, :HALF], vt[h, :, :HALF],
        )
        sums = [0.0, 0.0, 0.0, 0.0]

        def keys_done(t, factor, grad, lat, put):
            low = grad.astype(BF16)
            put(t, dot(factor, low, NT))
            sums[t] = sums[t] + fold(dot(lat, low))

        def queries_done(t, factor, grad_t, lat, put):
            put(t, dot(factor, grad_t))
            sums[t] = sums[t] + fold(dot(lat, grad_t, NT))

        def lat_of(t, at):
            return lat_low[32 * t : 32 * t + 32, at : at + HALF]

        def put_at(at):
            def put(t, value):
                grads[RANK * t : RANK * (t + 1), at : at + HALF] += value
            return put

        def put_back(t, value):
            for b in range(4):
                back[b // 2, b % 2, RANK * (t - 1) : RANK * t] += value[:, HD * b : HD * (b + 1)]

        for at, with_off in ((first_at, False), (last_at, True)):
            own = slice(at, at + HALF)
            keys, values = ka[h, own, :], va[h, own, :]
            keys_t, values_t = kt[h, :, own], vt[h, :, own]
            query, upstream = qa[h, own, :], ua[h, own, :]
            ahead = 0
            if with_off:
                ahead = HALF
                keys = jnp.concatenate([off_k, keys], axis=0)
                values = jnp.concatenate([off_v, values], axis=0)
                keys_t = jnp.concatenate([off_kt, keys_t], axis=1)
                values_t = jnp.concatenate([off_vt, values_t], axis=1)
            results = []
            for c in range(2):
                length = ahead + CHUNK * (c + 1)
                here = slice(CHUNK * c, CHUNK * (c + 1))
                results.append(
                    chunk_scores(
                        keys[:length], values[:length], keys_t[:, :length], values_t[:, :length],
                        query[here], upstream[here],
                    )
                )
            short = ahead + CHUNK
            (p0, s0, c0, q0), (p1, s1, c1, q1) = results

            def over_queries(early, late, rows):
                return jnp.concatenate(
                    [
                        dot(early, rows[:CHUNK]) + dot(late[:short], rows[CHUNK:]),
                        dot(late[short:], rows[CHUNK:]),
                    ],
                    axis=0,
                )

            grad_keys = over_queries(s0, s1, query)
            grad_values = over_queries(p0, p1, upstream)
            queries_done(0, uq, jnp.concatenate([q0, q1], axis=1), lat_of(0, at), put_at(at))
            queries_done(3, od, jnp.concatenate([c0, c1], axis=1), lat_of(3, at), put_at(at))
            for t, factor, grad in ((1, uk, grad_keys), (2, uv, grad_values)):
                keys_done(t, factor, grad[ahead:], lat_of(t, at), put_at(at))
                if with_off and off is None:
                    keys_done(t, factor, grad[:ahead], lat_of(t, 0), put_at(0))
                elif with_off:
                    keys_done(t, factor, grad[:ahead], prev_low[32 * t - 32 : 32 * t, :], put_back)
        for t in range(4):
            up_sum[slot, RANK * t : RANK * (t + 1)] = sums[t]

    def back_copy(c):
        return remote(
            back.at[c], back_in.at[core], back_send.at[c], back_recv.at[core],
            {"ctx": before, "head": y * 2 + c},
        )

    def both_kinds(i, carry):
        h = head_of[0] + i * (head_of[1] - head_of[0])
        still = head_of[2] + i * (head_of[3] - head_of[2])
        with jax.named_scope("wait_keys"):
            remote(kv_stage.at[i], kv_in.at[i], kv_send.at[i], kv_recv.at[i], {"ctx": after}).wait_recv()
        off_k = (kv_in[i, 0].astype(F32) + dot(prev_cols[...], prev_up[0, h])).astype(BF16)
        off_v = (kv_in[i, 1].astype(F32) + dot(prev_cols[...], prev_up[1, h])).astype(BF16)
        with jax.named_scope("attend_shifted"):
            attend(i, h, HALF, (off_k, off_v, off_k.T, off_v.T))

        @pl.when(i == 1)
        def _():
            for c in range(2):
                back_copy(c).start()

        with jax.named_scope("attend_still"):
            attend(2 + i, still, 0, None)
        return carry

    lax.fori_loop(0, 2, both_kinds, 0)

    with jax.named_scope("share_sum"):
        for b in range(8):
            part[1, place(b)] = grads[:, HD * b : HD * (b + 1)]

        def add_back():
            for c in range(2):
                remote(back.at[c], back_in.at[c], back_send.at[c], back_recv.at[c], sibling).wait_recv()
            none = jnp.zeros((RANK, HD), F32)
            return [0.0, 0.0] + [
                jnp.concatenate([none, back_in[0, i] + back_in[1, i], none], axis=0) for i in range(2)
            ]

        shares = sum_heads(1, add_back)
        next(shares)
        for h in range(4):
            cut[0, h] = up_sum[jnp.minimum(slot_of[h], 3)].astype(BF16)
        ups = sum_tokens(0)
        next(ups)
        next(shares)
        next(ups)
        next(shares)

    def down_gradients(owner):
        wide = jnp.concatenate([split_rows(2.0 * total[1, owner * 4 + i], 4).astype(BF16) for i in range(4)], axis=1)
        down = jnp.zeros((96, WIDTH), F32)
        last = jnp.zeros((32, WIDTH), F32)
        for j in range(2):
            rows = pl.ds(pl.multiple_of(owner * 256 + HALF * j, 256), 256)
            here = wide[:, 256 * j : 256 * (j + 1)]
            down = down + dot(here[:96], xb[rows, :])
            last = last + dot(here[96:], dob[rows, :])
        return jnp.concatenate([fold(down[32 * t : 32 * t + 32]) for t in range(3)] + [fold(last)], axis=0)

    with jax.named_scope("down_gradients"):
        down = down_gradients(core)
        next(shares)
        down = down + down_gradients(1 - core)
        for c in range(4):
            cut[1, c] = down[:, HD * c : HD * (c + 1)].astype(BF16)
    with jax.named_scope("token_sum"):
        downs = sum_tokens(1)
        next(downs)
        next(ups)
        next(downs)
        next(ups)
        next(downs)
        next(downs)
    for copy in sends:
        copy.wait_send()
    for c in range(2):
        back_copy(c).wait_send()


def on_device(
    inputs, q_base, k_base, v_base, d_out, d_ctx_base, flags,
    query_down_factor, up_q, key_down_factor, up_k, value_down_factor, up_v, down_o, output_up_factor,
):
    anywhere = pl.BlockSpec(memory_space=pl.ANY)
    vmem = pl.BlockSpec(memory_space=pltpu.VMEM)
    smem = pl.BlockSpec(memory_space=pltpu.SMEM)
    dma = pltpu.SemaphoreType.DMA
    v = pltpu.VMEM
    out = pl.pallas_call(
        kernel,
        out_shape=jax.ShapeDtypeStruct((2, 64, WIDTH), F32),
        in_specs=[anywhere] * 6 + [smem] + [anywhere] * 8,
        out_specs=vmem,
        scratch_shapes=[
            v((4, RANK, WIDTH), BF16), v((4, RANK, WIDTH), BF16),
            v((ROWS, WIDTH), BF16), *[v((4, ROWS, HD), BF16) for _ in range(3)],
            v((ROWS, WIDTH), BF16), v((4, ROWS, HD), BF16),
            v((2, 2, HALF, HD), BF16), v((2, 2, HALF, HD), BF16),
            v((2, 8, 64, HD), F32), v((2, 4, 64, HD), F32), v((2, 4, 64, HD), BF16),
            v((2, 3, 4, 64, HD), BF16), v((2, 8, 64, HD), F32),
            v((4, 32, HD), F32), v((128, 4 * WIDTH), BF16), v((4, 4, RANK, HD), BF16),
            v((2, 4, 64, HD), BF16), v((128, ROWS), BF16),
            v((64, HALF), BF16), v((HALF, 64), BF16),
            *[v((4, ROWS, HD), BF16) for _ in range(4)],
            *[v((4, HD, ROWS), BF16) for _ in range(2)],
            v((64, ROWS), F32), v((2, 2, 32, HD), F32), v((2, 2, 32, HD), F32), v((4, 64, HD), F32),
            v((2, 4, 64, HD), BF16), v((2, 3, 64, HD), BF16), v((2, 64, HD), BF16),
            v((2, 7, 64, HD), BF16), v((2, 64, HD), BF16), v((2, 4, 64, HD), BF16),
            dma((26,)), dma((2,)), dma((2,)), dma((2,)), dma((2,)), dma((2,)), dma((2,)),
            dma((2,)), dma((2,)), dma((2, 3)), dma((2, 3)), dma((2,)), dma((2,)),
            dma((2, 3)), dma((2, 3)), dma((2, 7)), dma((2, 7)), dma((2, 3)), dma((2, 3)),
        ],
        compiler_params=pltpu.CompilerParams(
            collective_id=0, has_side_effects=True, vmem_limit_bytes=56 * 1024 * 1024
        ),
    )(
        inputs[0], q_base[0], k_base[0], v_base[0], d_out[0], d_ctx_base[0], flags,
        query_down_factor, up_q, key_down_factor, up_k, value_down_factor, up_v, down_o, output_up_factor,
    )
    result = []
    for t in range(4):
        rows = slice(RANK * t, RANK * (t + 1))
        result += [out[1, rows], out[0, rows]]
    return (result[0], result[1], result[2], result[3], result[4], result[5], result[7], result[6])


def solution(mesh):
    tokens = P("dp", "ctx", "head")
    factor = P(None, "head")
    return jax.shard_map(
        on_device,
        mesh=mesh,
        in_specs=(tokens,) * 6 + (P("head"),) + (factor,) * 8,
        out_specs=(factor,) * 8,
        check_vma=False,
    )
```

```python
import functools
import math

import jax
import jax.numpy as jnp
from jax import lax
from jax.experimental import pallas as pl
from jax.experimental.pallas import tpu as pltpu
from jax.sharding import PartitionSpec as P

HD = 128
ROWS = 1024
HALF = 512
CHUNK = 256
STRIP = 64
RANK = 16
WIDTH = 512
NY, NZ, NX = 4, 8, 4
SCALE = 1.0 / math.sqrt(HD)
EXP_SCALE = SCALE * math.log2(math.e)
MESH = pl.DeviceIdType.MESH
F32 = jnp.float32
BF16 = jnp.bfloat16
NN = (((1,), (0,)), ((), ()))
NT = (((1,), (1,)), ((), ()))


def dot(a, b, dims=NN):
    return lax.dot_general(a, b, dims, preferred_element_type=F32)


def place(block):
    return (block // 2) % 2 * 4 + block % 2 + 2 * (block // 4)


def split_rows(wide, kinds):
    rows = []
    for t in range(kinds):
        part = wide[RANK * t : RANK * (t + 1)]
        high = part.astype(BF16).astype(F32)
        rows += [high, part - high]
    return jnp.concatenate(rows, axis=0)


def fold(pair):
    return pair[:RANK] + pair[RANK:]


def fold_strip(strip, op):
    strip = strip.reshape(STRIP // 8, 8, CHUNK)
    result = strip[0]
    for i in range(1, STRIP // 8):
        result = op(result, strip[i])
    return result


def merged(*lists):
    timed = [((i + 0.5) / len(steps), k, step) for k, steps in enumerate(lists) for i, step in enumerate(steps)]
    return [step for _, _, step in sorted(timed, key=lambda item: item[:2])]


def kernel(
    x_hbm, q_hbm, k_hbm, v_hbm, do_hbm, dc_hbm, flags,
    down_q_hbm, up_q_hbm, down_k_hbm, up_k_hbm, down_v_hbm, up_v_hbm, down_o_hbm, up_o_hbm,
    out_ref,
    firsts, seconds,
    xb, qb, kb, vb, dob, dcb,
    kv_stage, kv_in,
    part, sib_in, acc, y_in, total,
    lat_prev, up_pad, fac, prev_up, lat_low, prev_low, prev_cols,
    qa, ka, va, ua, kt, vt,
    grad_q, grad_k, grad_v, ctx_all, back_k, back_v, off_rows, off_cols,
    score, grad_prob, prob_low, grad_low,
    back, back_in, up_sum,
    cut, x_in, x_sum, z_in, z_all, x_all,
    load_sem, kv_send, kv_recv, lp_send, lp_recv, back_send, back_recv,
    sib_send, sib_recv, y_send, y_recv, fw_send, fw_recv,
    x1_send, x1_recv, z_send, z_recv, x2_send, x2_recv,
):
    ctx, head, dp = lax.axis_index("ctx"), lax.axis_index("head"), lax.axis_index("dp")
    y, core = head // 2, head % 2
    x_lo, z = ctx // NZ, ctx % NZ
    x = dp * 2 + x_lo
    sibling = {"head": y * 2 + (1 - core)}
    after = lax.rem(ctx + 1, 2 * NZ)
    before = lax.rem(ctx + 2 * NZ - 1, 2 * NZ)

    def y_peer(d):
        return {"head": lax.rem(y + d, NY) * 2 + core}

    def z_peer(d):
        return {"ctx": x_lo * NZ + lax.rem(z + d, NZ)}

    def x_peer(d):
        other = lax.rem(x + d, NX)
        return {"ctx": (other % 2) * NZ + z, "dp": other // 2}

    loads = []

    def load(*pairs):
        for source, target in pairs:
            copy = pltpu.make_async_copy(source, target, load_sem.at[len(loads)])
            copy.start()
            loads.append(copy)

    def by_head(source, target):
        return [(source.at[:, pl.ds(HD * h, HD)], target.at[h]) for h in range(4)]

    load(
        (down_q_hbm, firsts.at[0]), (down_k_hbm, firsts.at[1]), (down_v_hbm, firsts.at[2]), (up_o_hbm, firsts.at[3]),
        (x_hbm, xb), (do_hbm, dob),
        (up_q_hbm, seconds.at[0]), (up_k_hbm, seconds.at[1]), (up_v_hbm, seconds.at[2]), (down_o_hbm, seconds.at[3]),
        *by_head(k_hbm, kb), *by_head(v_hbm, vb),
    )

    barrier = pltpu.get_barrier_semaphore()
    peers = [sibling]
    peers += [y_peer(d) for d in range(1, NY)]
    peers += [z_peer(d) for d in range(1, NZ)]
    peers += [x_peer(d) for d in range(1, NX)]
    for near in (after, before):
        peers += [{"ctx": near}, {"ctx": near, "head": y * 2 + (1 - core)}]
    for peer in peers:
        pl.semaphore_signal(barrier, inc=1, device_id=peer, device_id_type=MESH)

    sends = []

    def remote(source, target, send_sem, recv_sem, peer):
        return pltpu.make_async_remote_copy(
            src_ref=source, dst_ref=target, send_sem=send_sem, recv_sem=recv_sem,
            device_id=peer, device_id_type=MESH,
        )

    def send(*args):
        copy = remote(*args)
        copy.start()
        sends.append(copy)

    f0, f1, f2, f3 = (flags[h] for h in range(4))
    head_of = (
        (1 - f0) * (2 - f1),
        3 * f3 + (1 - f3) * (1 + f2),
        f0 * (1 + f1),
        3 * (1 - f3) + f3 * (2 - f2),
    )
    slot_of = (
        2 - 2 * f0,
        f1 * f0 + (1 - f1) * (2 + 1 - f0),
        f2 * (f0 + f1) + (1 - f2) * (4 - f0 - f1),
        f3 + (1 - f3) * 3,
    )

    def own_latents(owner):
        first = firsts[...].reshape(4 * RANK, WIDTH)
        for j in range(2):
            rows = pl.ds(pl.multiple_of(owner * 256 + HALF * j, 256), 256)
            lat_part = dot(first[: 3 * RANK], xb[rows, :], NT)
            mix_part = dot(first[3 * RANK :], dob[rows, :], NT)
            for k in range(2):
                part[0, owner * 4 + 2 * j + k, : 3 * RANK] = lat_part[:, HD * k : HD * (k + 1)]
                part[0, owner * 4 + 2 * j + k, 3 * RANK :] = mix_part[:, HD * k : HD * (k + 1)]

    for copy in loads[:6]:
        copy.wait()
    with jax.named_scope("own_latents"):
        own_latents(1 - core)
    with jax.named_scope("entry_barrier"):
        pl.semaphore_wait(barrier, len(peers))

    mine = core * 4
    other = (1 - core) * 4

    def sum_heads(p, late=None):
        pair = (part.at[p, pl.ds(other, 4)], sib_in.at[p], sib_send.at[p], sib_recv.at[p], sibling)
        send(*pair)
        yield
        remote(*pair).wait_recv()
        extra = [0.0] * 4 if late is None else late()
        for i in range(4):
            acc[p, i] = (part[p, mine + i] + sib_in[p, i] + extra[i]).astype(BF16)
        shares = [(acc.at[p], y_in.at[p, d - 1], y_send.at[p, d - 1], y_recv.at[p, d - 1], y_peer(d)) for d in range(1, NY)]
        for share in shares:
            send(*share)
        yield
        for share in shares:
            remote(*share).wait_recv()
        for i in range(4):
            summed = acc[p, i].astype(F32)
            for d in range(1, NY):
                summed = summed + y_in[p, d - 1, i].astype(F32)
            total[p, mine + i] = summed
        own = total.at[p, pl.ds(mine, 4)]
        send(own, own, fw_send.at[p], fw_recv.at[p], sibling)
        yield
        came = total.at[p, pl.ds(other, 4)]
        remote(came, came, fw_send.at[p], fw_recv.at[p], sibling).wait_recv()
        yield

    def sum_tokens(e):
        for d in range(1, NX):
            send(cut.at[e, lax.rem(x + d, NX)], x_in.at[e, d - 1], x1_send.at[e, d - 1], x1_recv.at[e, d - 1], x_peer(d))
        yield
        summed = cut[e, x].astype(F32)
        for d in range(1, NX):
            remote(cut.at[e, 0], x_in.at[e, d - 1], x1_send.at[e, d - 1], x1_recv.at[e, d - 1], x_peer(d)).wait_recv()
            summed = summed + x_in[e, d - 1].astype(F32)
        x_sum[e] = summed.astype(BF16)
        shares = [(x_sum.at[e], z_in.at[e, d - 1], z_send.at[e, d - 1], z_recv.at[e, d - 1], z_peer(d)) for d in range(1, NZ)]
        for share in shares:
            send(*share)
        yield
        summed = x_sum[e].astype(F32)
        for d, share in enumerate(shares):
            remote(*share).wait_recv()
            summed = summed + z_in[e, d].astype(F32)
        z_all[e] = summed.astype(BF16)
        for d in range(1, NX):
            send(z_all.at[e], x_all.at[e, x], x2_send.at[e, d - 1], x2_recv.at[e, d - 1], x_peer(d))
        x_all[e, x] = z_all[e]
        yield
        for d in range(1, NX):
            came = x_all.at[e, lax.rem(x + NX - d, NX)]
            remote(z_all.at[e], came, x2_send.at[e, d - 1], x2_recv.at[e, d - 1], x_peer(d)).wait_recv()
        for c in range(4):
            out_ref[e, :, HD * c : HD * (c + 1)] = x_all[e, c].astype(F32)
        yield

    latents = sum_heads(0)
    next(latents)
    with jax.named_scope("own_latents"):
        own_latents(core)
    with jax.named_scope("latent_sum"):
        next(latents)

    with jax.named_scope("stage_keys"):
        for copy in loads[10:18]:
            copy.wait()
        for s in range(2):
            for i, base in enumerate((kb, vb)):
                kv_stage[s, i] = base[head_of[s], HALF:, :]
            send(kv_stage.at[s], kv_in.at[s], kv_send.at[s], kv_recv.at[s], {"ctx": after})

    load(*by_head(q_hbm, qb), *by_head(dc_hbm, dcb))
    for copy in loads[6:10]:
        copy.wait()
    up_pad[...] = jnp.zeros_like(up_pad)
    for t, factor in enumerate(seconds[t] for t in range(4)):
        for copy_at in (0, RANK):
            up_pad[32 * t + copy_at : 32 * t + copy_at + RANK, WIDTH * t : WIDTH * (t + 1)] = factor
        for h in range(4):
            fac[t, h] = factor[:, HD * h : HD * (h + 1)]
    for t in range(2):
        for h in range(4):
            at = WIDTH * (1 + t) + HD * h
            prev_up[t, h] = up_pad[32:96, at : at + HD]

    with jax.named_scope("latent_sum"):
        next(latents)

    def adapt(i, owner):
        b = owner * 2 + i % 2 + 4 * (i // 2)
        rows = pl.ds(pl.multiple_of(b * HD, HD), HD)
        both = split_rows(2.0 * total[0, owner * 4 + i], 4)
        lat_low[:, rows] = both.astype(BF16)
        extra = dot(both.T.astype(BF16), up_pad[...])
        for t, (base, full, turned) in enumerate(
            ((qb, qa, None), (kb, ka, kt), (vb, va, vt), (dcb, ua, None))
        ):
            for h in range(4):
                at = WIDTH * t + HD * h
                low = (base[h, rows, :].astype(F32) + extra[:, at : at + HD]).astype(BF16)
                full[h, rows, :] = low
                if turned is not None:
                    turned[h, :, rows] = low.T
        return owner

    for copy in loads[18:]:
        copy.wait()
    with jax.named_scope("adapt"):
        lax.fori_loop(0, 4, adapt, core)
    with jax.named_scope("latent_sum"):
        next(latents)
    for c in range(2):
        send(
            total.at[0, pl.ds(4 * c + 2, 2), pl.ds(RANK, 2 * RANK)], lat_prev.at[pl.ds(2 * c, 2)],
            lp_send.at[c], lp_recv.at[c], {"ctx": after},
        )
    with jax.named_scope("adapt"):
        lax.fori_loop(0, 4, adapt, 1 - core)
        for c in range(2):
            remote(
                total.at[0, pl.ds(4 * c + 2, 2), pl.ds(RANK, 2 * RANK)], lat_prev.at[pl.ds(2 * c, 2)],
                lp_send.at[c], lp_recv.at[c], {"ctx": after},
            ).wait_recv()
        for b in range(4):
            both = split_rows(2.0 * lat_prev[b], 2)
            prev_low[:, HD * b : HD * (b + 1)] = both.astype(BF16)
            prev_cols[HD * b : HD * (b + 1), :] = both.T.astype(BF16)

    def chunk(j, slot, at, with_off, c, sums):
        h = head_of[slot]
        off = slot if slot < 2 else None
        s, g, p, ds = (ref.at[j % 2] for ref in (score, grad_prob, prob_low, grad_low))
        ahead = HALF if with_off else 0
        length = ahead + CHUNK * (c + 1)
        strips = length // STRIP
        here = slice(at + CHUNK * c, at + CHUNK * (c + 1))
        held = {}

        def key_rows(t, b):
            first = CHUNK * b
            if first >= ahead:
                return (ka, va)[t][h, at + first - ahead : at + first - ahead + CHUNK, :]
            if off is not None:
                return off_rows[off, t, first : first + CHUNK]
            return (ka, va)[t][h, first : first + CHUNK, :]

        def key_cols(t):
            own = (kt, vt)[t][h, :, at : at + length - ahead]
            if not with_off:
                return own
            early = off_cols[off, t] if off is not None else (kt, vt)[t][h, :, :HALF]
            return jnp.concatenate([early, own], axis=1)

        def strip(i):
            return slice(STRIP * i, STRIP * (i + 1))

        def scores_of(b):
            s[CHUNK * b : CHUNK * (b + 1), :] = dot(key_rows(0, b), qa[h, here, :], NT)

        def grad_probs_of(b):
            g[CHUNK * b : CHUNK * (b + 1), :] = dot(key_rows(1, b), ua[h, here, :], NT)

        def causal(i):
            value = s[strip(i), :]
            first = STRIP * i - (length - CHUNK)
            if first < 0:
                return value
            key = lax.broadcasted_iota(jnp.int32, value.shape, 0) + first
            return jnp.where(key <= lax.broadcasted_iota(jnp.int32, value.shape, 1), value, -jnp.inf)

        def peaks(i):
            peak = fold_strip(causal(i), jnp.maximum)
            held["peak"] = peak if i == 0 else jnp.maximum(held["peak"], peak)

        def weigh(i):
            if i == 0:
                held["peak"] = jnp.max(held["peak"], axis=0, keepdims=True)
                held["sum"] = held["center"] = jnp.zeros((8, CHUNK), F32)
            weights = jnp.exp2((causal(i) - held["peak"]) * EXP_SCALE)
            s[strip(i), :] = weights
            held["sum"] = held["sum"] + fold_strip(weights, jnp.add)
            held["center"] = held["center"] + fold_strip(weights * g[strip(i), :], jnp.add)

        def finish(i):
            if i == 0:
                held["inverse"] = 1.0 / jnp.sum(held["sum"], axis=0, keepdims=True)
                held["center"] = jnp.sum(held["center"], axis=0, keepdims=True) * held["inverse"]
                held["scaled"] = held["inverse"] * SCALE
            weights = s[strip(i), :]
            p[strip(i), :] = (weights * held["inverse"]).astype(BF16)
            ds[strip(i), :] = ((weights * held["scaled"]) * (g[strip(i), :] - held["center"])).astype(BF16)

        def query_side():
            grad_q[slot, :, here] = dot(key_cols(0), ds[:length, :]).astype(BF16)

        def context_side():
            ctx_all[slot, :, here] = dot(key_cols(1), p[:length, :]).astype(BF16)

        def key_side(t, b):
            low, rows = ((ds, qa), (p, ua))[t]
            value = dot(low[CHUNK * b : CHUNK * (b + 1), :], rows[h, here, :])
            name = (t, with_off, b)
            sums[name] = sums[name] + value if name in sums else value

        blocks = range(length // CHUNK)
        before_it = [functools.partial(f, b) for b in blocks for f in (scores_of, grad_probs_of)]
        middle = [functools.partial(f, i) for f in (peaks, weigh, finish) for i in range(strips)]
        after_it = [query_side, context_side] + [functools.partial(key_side, t, b) for b in blocks for t in (0, 1)]
        return before_it, middle, after_it

    def keys_done(slot, sums):
        for t, (grad, away) in enumerate(((grad_k, back_k), (grad_v, back_v))):
            for b in range(2):
                early, late = slice(CHUNK * b, CHUNK * (b + 1)), slice(HALF + CHUNK * b, HALF + CHUNK * (b + 1))
                first, off, last = sums[t, False, b], sums[t, True, b], sums[t, True, b + 2]
                if slot < 2:
                    away[slot, early] = off.astype(BF16)
                    grad[slot, early] = last.astype(BF16)
                    grad[slot, late] = first.astype(BF16)
                else:
                    grad[slot, early] = (first + off).astype(BF16)
                    grad[slot, late] = last.astype(BF16)

    def factors(t, slots):
        return jnp.concatenate([fac[t, head_of[slot]] for slot in slots], axis=1)

    def stacked(ref, slots):
        return jnp.concatenate([ref[slot] for slot in slots], axis=0)

    def beside(ref, slots):
        return jnp.concatenate([ref[slot] for slot in slots], axis=1)

    def projections(slots):
        return [
            dot(factors(0, slots), stacked(grad_q, slots)),
            dot(factors(1, slots), beside(grad_k, slots), NT),
            dot(factors(2, slots), beside(grad_v, slots), NT),
            dot(factors(3, slots), stacked(ctx_all, slots)),
        ]

    def back_copy(c):
        return remote(
            back.at[c], back_in.at[core], back_send.at[c], back_recv.at[core],
            {"ctx": before, "head": y * 2 + c},
        )

    def keys_from_before(slot):
        remote(
            kv_stage.at[slot], kv_in.at[slot], kv_send.at[slot], kv_recv.at[slot], {"ctx": after}
        ).wait_recv()
        for t in range(2):
            extra = dot(prev_cols[...], prev_up[t, head_of[slot]])
            low = (kv_in[slot, t].astype(F32) + extra).astype(BF16)
            off_rows[slot, t] = low
            off_cols[slot, t] = low.T

    def send_back():
        for t, ref in ((1, back_k), (2, back_v)):
            value = dot(factors(t, (0, 1)), beside(ref, (0, 1)), NT)
            for b in range(4):
                back[b // 2, b % 2, RANK * (t - 1) : RANK * t] = value[:, HD * b : HD * (b + 1)]
        for c in range(2):
            back_copy(c).start()

    with jax.named_scope("attend"):
        chunks, at_start, at_end, shares = [], {}, {}, []
        all_sums = [{}, {}, {}, {}]
        order = [(0, False), (1, False), (0, True), (1, True), (2, False), (2, True), (3, False), (3, True)]
        for slot, with_off in order:
            first_at = HALF if slot < 2 else 0
            if slot < 2 and with_off:
                at_start[len(chunks)] = functools.partial(keys_from_before, slot)
            for c in range(2):
                at = HALF - first_at if with_off else first_at
                chunks.append(chunk(len(chunks), slot, at, with_off, c, all_sums[slot]))
            if with_off:
                at_end[len(chunks) - 1] = functools.partial(keys_done, slot, all_sums[slot])
        count = len(chunks)
        for step in chunks[0][0]:
            step()
        for j in range(count + 1):
            if j + 1 in at_start:
                at_start[j + 1]()
            lists = [chunks[j][1]] if j < count else []
            lists += [chunks[j + 1][0]] if j + 1 < count else []
            lists += [chunks[j - 1][2]] if j else []
            for step in merged(*lists):
                step()
            if j - 1 in at_end:
                at_end[j - 1]()
            if j - 1 == 7:
                send_back()
            if j == count - 1:
                shares = projections((0, 1))
        wide = jnp.concatenate([a + b for a, b in zip(shares, projections((2, 3)))], axis=0)

    with jax.named_scope("share_sum"):
        for b in range(8):
            part[1, place(b)] = wide[:, HD * b : HD * (b + 1)]

        def add_back():
            for c in range(2):
                remote(back.at[c], back_in.at[c], back_send.at[c], back_recv.at[c], sibling).wait_recv()
            none = jnp.zeros((RANK, HD), F32)
            return [0.0, 0.0] + [
                jnp.concatenate([none, back_in[0, i] + back_in[1, i], none], axis=0) for i in range(2)
            ]

        shares = sum_heads(1, add_back)
        next(shares)
        next(shares)
        every = (0, 1, 2, 3)
        up_rows = [
            fold(dot(lat_low[:32, :], stacked(grad_q, every), NT)),
            fold(dot(lat_low[32:64, :], beside(grad_k, every))),
            fold(dot(lat_low[64:96, :], beside(grad_v, every))),
            fold(dot(lat_low[96:, :], stacked(ctx_all, every), NT)),
        ]
        for t, ref in ((1, back_k), (2, back_v)):
            extra = fold(dot(prev_low[32 * t - 32 : 32 * t, :], beside(ref, (0, 1))))
            up_rows[t] = up_rows[t] + jnp.concatenate([extra, jnp.zeros_like(extra)], axis=1)
        up_rows = jnp.concatenate(up_rows, axis=0)
        for slot in every:
            up_sum[slot] = up_rows[:, HD * slot : HD * (slot + 1)]
        for h in range(4):
            cut[0, h] = up_sum[jnp.minimum(slot_of[h], 3)].astype(BF16)
        ups = sum_tokens(0)
        next(ups)
        next(shares)
        next(ups)

    def down_gradients(owner):
        wide = jnp.concatenate([split_rows(2.0 * total[1, owner * 4 + i], 4).astype(BF16) for i in range(4)], axis=1)
        down = jnp.zeros((96, WIDTH), F32)
        last = jnp.zeros((32, WIDTH), F32)
        for j in range(2):
            rows = pl.ds(pl.multiple_of(owner * 256 + HALF * j, 256), 256)
            here = wide[:, 256 * j : 256 * (j + 1)]
            down = down + dot(here[:96], xb[rows, :])
            last = last + dot(here[96:], dob[rows, :])
        return jnp.concatenate([fold(down[32 * t : 32 * t + 32]) for t in range(3)] + [fold(last)], axis=0)

    with jax.named_scope("down_gradients"):
        down = down_gradients(core)
        next(shares)
        down = down + down_gradients(1 - core)
        for c in range(4):
            cut[1, c] = down[:, HD * c : HD * (c + 1)].astype(BF16)
    with jax.named_scope("token_sum"):
        downs = sum_tokens(1)
        next(downs)
        next(ups)
        next(downs)
        next(ups)
        next(downs)
        next(downs)
    for copy in sends:
        copy.wait_send()
    for c in range(2):
        back_copy(c).wait_send()


def on_device(
    inputs, q_base, k_base, v_base, d_out, d_ctx_base, flags,
    query_down_factor, up_q, key_down_factor, up_k, value_down_factor, up_v, down_o, output_up_factor,
):
    anywhere = pl.BlockSpec(memory_space=pl.ANY)
    vmem = pl.BlockSpec(memory_space=pltpu.VMEM)
    smem = pl.BlockSpec(memory_space=pltpu.SMEM)
    dma = pltpu.SemaphoreType.DMA
    v = pltpu.VMEM
    out = pl.pallas_call(
        kernel,
        out_shape=jax.ShapeDtypeStruct((2, 64, WIDTH), F32),
        in_specs=[anywhere] * 6 + [smem] + [anywhere] * 8,
        out_specs=vmem,
        scratch_shapes=[
            v((4, RANK, WIDTH), BF16), v((4, RANK, WIDTH), BF16),
            v((ROWS, WIDTH), BF16), *[v((4, ROWS, HD), BF16) for _ in range(3)],
            v((ROWS, WIDTH), BF16), v((4, ROWS, HD), BF16),
            v((2, 2, HALF, HD), BF16), v((2, 2, HALF, HD), BF16),
            v((2, 8, 64, HD), F32), v((2, 4, 64, HD), F32), v((2, 4, 64, HD), BF16),
            v((2, 3, 4, 64, HD), BF16), v((2, 8, 64, HD), F32),
            v((4, 32, HD), F32), v((128, 4 * WIDTH), BF16), v((4, 4, RANK, HD), BF16),
            v((2, 4, 64, HD), BF16), v((128, ROWS), BF16),
            v((64, HALF), BF16), v((HALF, 64), BF16),
            *[v((4, ROWS, HD), BF16) for _ in range(4)],
            *[v((4, HD, ROWS), BF16) for _ in range(2)],
            v((4, HD, ROWS), BF16), v((4, ROWS, HD), BF16), v((4, ROWS, HD), BF16), v((4, HD, ROWS), BF16),
            v((2, HALF, HD), BF16), v((2, HALF, HD), BF16), v((2, 2, HALF, HD), BF16), v((2, 2, HD, HALF), BF16),
            v((2, ROWS, CHUNK), F32), v((2, ROWS, CHUNK), F32), v((2, ROWS, CHUNK), BF16), v((2, ROWS, CHUNK), BF16),
            v((2, 2, 32, HD), F32), v((2, 2, 32, HD), F32), v((4, 64, HD), F32),
            v((2, 4, 64, HD), BF16), v((2, 3, 64, HD), BF16), v((2, 64, HD), BF16),
            v((2, 7, 64, HD), BF16), v((2, 64, HD), BF16), v((2, 4, 64, HD), BF16),
            dma((26,)), dma((2,)), dma((2,)), dma((2,)), dma((2,)), dma((2,)), dma((2,)),
            dma((2,)), dma((2,)), dma((2, 3)), dma((2, 3)), dma((2,)), dma((2,)),
            dma((2, 3)), dma((2, 3)), dma((2, 7)), dma((2, 7)), dma((2, 3)), dma((2, 3)),
        ],
        compiler_params=pltpu.CompilerParams(
            collective_id=0, has_side_effects=True, vmem_limit_bytes=56 * 1024 * 1024
        ),
    )(
        inputs[0], q_base[0], k_base[0], v_base[0], d_out[0], d_ctx_base[0], flags,
        query_down_factor, up_q, key_down_factor, up_k, value_down_factor, up_v, down_o, output_up_factor,
    )
    result = []
    for t in range(4):
        rows = slice(RANK * t, RANK * (t + 1))
        result += [out[1, rows], out[0, rows]]
    return (result[0], result[1], result[2], result[3], result[4], result[5], result[7], result[6])


def solution(mesh):
    tokens = P("dp", "ctx", "head")
    factor = P(None, "head")
    return jax.shard_map(
        on_device,
        mesh=mesh,
        in_specs=(tokens,) * 6 + (P("head"),) + (factor,) * 8,
        out_specs=(factor,) * 8,
        check_vma=False,
    )
```

```python
import functools
import math

import jax
import jax.numpy as jnp
from jax import lax
from jax.experimental import pallas as pl
from jax.experimental.pallas import tpu as pltpu
from jax.sharding import PartitionSpec as P

HD = 128
ROWS = 1024
HALF = 512
CHUNK = 256
STRIP = 64
RANK = 16
WIDTH = 512
NY, NZ, NX = 4, 8, 4
Y_ORDER = X_ORDER = (2, 1, 3)
Z_ORDER = (4, 3, 5, 2, 6, 1, 7)
SCALE = 1.0 / math.sqrt(HD)
EXP_SCALE = SCALE * math.log2(math.e)
MESH = pl.DeviceIdType.MESH
F32 = jnp.float32
BF16 = jnp.bfloat16
NN = (((1,), (0,)), ((), ()))
NT = (((1,), (1,)), ((), ()))


def dot(a, b, dims=NN):
    return lax.dot_general(a, b, dims, preferred_element_type=F32)


def place(block):
    return (block // 2) % 2 * 4 + block % 2 + 2 * (block // 4)


def split_rows(wide, kinds):
    rows = []
    for t in range(kinds):
        part = wide[RANK * t : RANK * (t + 1)]
        high = part.astype(BF16).astype(F32)
        rows += [high, part - high]
    return jnp.concatenate(rows, axis=0)


def fold(pair):
    return pair[:RANK] + pair[RANK:]


def fold_strip(strip, op):
    strip = strip.reshape(STRIP // 8, 8, CHUNK)
    result = strip[0]
    for i in range(1, STRIP // 8):
        result = op(result, strip[i])
    return result


def merged(*lists):
    timed = [((i + 0.5) / len(steps), k, step) for k, steps in enumerate(lists) for i, step in enumerate(steps)]
    return [step for _, _, step in sorted(timed, key=lambda item: item[:2])]


def kernel(
    x_hbm, q_hbm, k_hbm, v_hbm, do_hbm, dc_hbm, flags_hbm,
    down_q_hbm, up_q_hbm, down_k_hbm, up_k_hbm, down_v_hbm, up_v_hbm, down_o_hbm, up_o_hbm,
    out_ref,
    flags, firsts, seconds,
    xb, qb, kb, vb, dob, dcb,
    kv_stage, kv_in,
    part, sib_in, acc, y_in, total,
    lat_prev, up_pad, fac, prev_up, lat_low, prev_low, prev_cols,
    qa, ka, va, ua, kt, vt,
    grad_q, grad_k, grad_v, ctx_all, back_k, back_v, off_rows, off_cols,
    score, grad_prob, prob_low, grad_low,
    back, back_in, up_sum,
    cut, x_in, x_sum, z_in, z_all, x_all,
    load_sem, kv_send, kv_recv, lp_send, lp_recv, back_send, back_recv,
    sib_send, sib_recv, y_send, y_recv, fw_send, fw_recv,
    x1_send, x1_recv, z_send, z_recv, x2_send, x2_recv,
):
    ctx, head, dp = lax.axis_index("ctx"), lax.axis_index("head"), lax.axis_index("dp")
    y, core = head // 2, head % 2
    x_lo, z = ctx // NZ, ctx % NZ
    x = dp * 2 + x_lo
    sibling = {"head": y * 2 + (1 - core)}
    after = lax.rem(ctx + 1, 2 * NZ)
    before = lax.rem(ctx + 2 * NZ - 1, 2 * NZ)

    def y_peer(d):
        return {"head": lax.rem(y + d, NY) * 2 + core}

    def z_peer(d):
        return {"ctx": x_lo * NZ + lax.rem(z + d, NZ)}

    def x_peer(d):
        other = lax.rem(x + d, NX)
        return {"ctx": (other % 2) * NZ + z, "dp": other // 2}

    loads = []

    def load(*pairs):
        for source, target in pairs:
            copy = pltpu.make_async_copy(source, target, load_sem.at[len(loads)])
            copy.start()
            loads.append(copy)

    def by_head(source, target):
        return [(source.at[:, pl.ds(HD * h, HD)], target.at[h]) for h in range(4)]

    def rows_of(owner, j):
        return pl.ds(pl.multiple_of(owner * 256 + HALF * j, 256), 256)

    def by_owner(owner):
        rows = [rows_of(owner, j) for j in range(2)]
        return [(source.at[r], target.at[r]) for source, target in ((x_hbm, xb), (do_hbm, dob)) for r in rows]

    load(
        (down_q_hbm, firsts.at[0]), (down_k_hbm, firsts.at[1]), (down_v_hbm, firsts.at[2]), (up_o_hbm, firsts.at[3]),
        *by_owner(1 - core), *by_owner(core), (flags_hbm, flags),
    )

    barrier = pltpu.get_barrier_semaphore()
    peers = [sibling]
    peers += [y_peer(d) for d in range(1, NY)]
    peers += [z_peer(d) for d in range(1, NZ)]
    peers += [x_peer(d) for d in range(1, NX)]
    for near in (after, before):
        peers += [{"ctx": near}, {"ctx": near, "head": y * 2 + (1 - core)}]
    for peer in peers:
        pl.semaphore_signal(barrier, inc=1, device_id=peer, device_id_type=MESH)

    sends = []

    def remote(source, target, send_sem, recv_sem, peer):
        return pltpu.make_async_remote_copy(
            src_ref=source, dst_ref=target, send_sem=send_sem, recv_sem=recv_sem,
            device_id=peer, device_id_type=MESH,
        )

    def send(*args):
        copy = remote(*args)
        copy.start()
        sends.append(copy)

    def own_latents(owner):
        first = firsts[...].reshape(4 * RANK, WIDTH)
        for j in range(2):
            rows = rows_of(owner, j)
            lat_part = dot(first[: 3 * RANK], xb[rows, :], NT)
            mix_part = dot(first[3 * RANK :], dob[rows, :], NT)
            for k in range(2):
                part[0, owner * 4 + 2 * j + k, : 3 * RANK] = lat_part[:, HD * k : HD * (k + 1)]
                part[0, owner * 4 + 2 * j + k, 3 * RANK :] = mix_part[:, HD * k : HD * (k + 1)]

    for copy in loads[:8]:
        copy.wait()
    with jax.named_scope("own_latents"):
        own_latents(1 - core)
    with jax.named_scope("entry_barrier"):
        pl.semaphore_wait(barrier, len(peers))

    mine = core * 4
    other = (1 - core) * 4

    def sum_heads(p, late=None):
        pair = (part.at[p, pl.ds(other, 4)], sib_in.at[p], sib_send.at[p], sib_recv.at[p], sibling)
        send(*pair)
        yield
        remote(*pair).wait_recv()
        extra = [0.0] * 4 if late is None else late()
        for i in range(4):
            acc[p, i] = (part[p, mine + i] + sib_in[p, i] + extra[i]).astype(BF16)
        shares = [(acc.at[p], y_in.at[p, d - 1], y_send.at[p, d - 1], y_recv.at[p, d - 1], y_peer(d)) for d in Y_ORDER]
        for share in shares:
            send(*share)
        yield
        for share in shares:
            remote(*share).wait_recv()
        for i in range(4):
            summed = acc[p, i].astype(F32)
            for d in range(1, NY):
                summed = summed + y_in[p, d - 1, i].astype(F32)
            total[p, mine + i] = summed
        own = total.at[p, pl.ds(mine, 4)]
        send(own, own, fw_send.at[p], fw_recv.at[p], sibling)
        yield
        came = total.at[p, pl.ds(other, 4)]
        remote(came, came, fw_send.at[p], fw_recv.at[p], sibling).wait_recv()
        yield

    def sum_tokens(e):
        for d in X_ORDER:
            send(cut.at[e, lax.rem(x + d, NX)], x_in.at[e, d - 1], x1_send.at[e, d - 1], x1_recv.at[e, d - 1], x_peer(d))
        yield
        summed = cut[e, x].astype(F32)
        for d in range(1, NX):
            remote(cut.at[e, 0], x_in.at[e, d - 1], x1_send.at[e, d - 1], x1_recv.at[e, d - 1], x_peer(d)).wait_recv()
            summed = summed + x_in[e, d - 1].astype(F32)
        x_sum[e] = summed.astype(BF16)
        shares = [(x_sum.at[e], z_in.at[e, d - 1], z_send.at[e, d - 1], z_recv.at[e, d - 1], z_peer(d)) for d in Z_ORDER]
        for share in shares:
            send(*share)
        yield
        summed = x_sum[e].astype(F32)
        for share in shares:
            remote(*share).wait_recv()
        for d in range(1, NZ):
            summed = summed + z_in[e, d - 1].astype(F32)
        z_all[e] = summed.astype(BF16)
        for d in X_ORDER:
            send(z_all.at[e], x_all.at[e, x], x2_send.at[e, d - 1], x2_recv.at[e, d - 1], x_peer(d))
        x_all[e, x] = z_all[e]
        yield
        for d in range(1, NX):
            came = x_all.at[e, lax.rem(x + NX - d, NX)]
            remote(z_all.at[e], came, x2_send.at[e, d - 1], x2_recv.at[e, d - 1], x_peer(d)).wait_recv()
        for c in range(4):
            out_ref[e, :, HD * c : HD * (c + 1)] = x_all[e, c].astype(F32)
        yield

    latents = sum_heads(0)
    next(latents)
    load(
        *by_head(k_hbm, kb), *by_head(v_hbm, vb),
        (up_q_hbm, seconds.at[0]), (up_k_hbm, seconds.at[1]), (up_v_hbm, seconds.at[2]), (down_o_hbm, seconds.at[3]),
    )
    for copy in loads[8:13]:
        copy.wait()
    with jax.named_scope("own_latents"):
        own_latents(core)
    with jax.named_scope("latent_sum"):
        next(latents)

    f0, f1, f2, f3 = (flags[h] for h in range(4))
    head_of = (
        (1 - f0) * (2 - f1),
        3 * f3 + (1 - f3) * (1 + f2),
        f0 * (1 + f1),
        3 * (1 - f3) + f3 * (2 - f2),
    )
    slot_of = (
        2 - 2 * f0,
        f1 * f0 + (1 - f1) * (2 + 1 - f0),
        f2 * (f0 + f1) + (1 - f2) * (4 - f0 - f1),
        f3 + (1 - f3) * 3,
    )

    with jax.named_scope("stage_keys"):
        for copy in loads[13:21]:
            copy.wait()
        for s in range(2):
            for i, base in enumerate((kb, vb)):
                kv_stage[s, i] = base[head_of[s], HALF:, :]
            send(kv_stage.at[s], kv_in.at[s], kv_send.at[s], kv_recv.at[s], {"ctx": after})

    load(*by_head(q_hbm, qb), *by_head(dc_hbm, dcb))
    for copy in loads[21:25]:
        copy.wait()
    up_pad[...] = jnp.zeros_like(up_pad)
    for t, factor in enumerate(seconds[t] for t in range(4)):
        for copy_at in (0, RANK):
            up_pad[32 * t + copy_at : 32 * t + copy_at + RANK, WIDTH * t : WIDTH * (t + 1)] = factor
        for h in range(4):
            fac[t, h] = factor[:, HD * h : HD * (h + 1)]
    for t in range(2):
        for h in range(4):
            at = WIDTH * (1 + t) + HD * h
            prev_up[t, h] = up_pad[32:96, at : at + HD]

    with jax.named_scope("latent_sum"):
        next(latents)

    def adapt(owner):
        for j in range(2):
            rows = rows_of(owner, j)
            both = jnp.concatenate([split_rows(2.0 * total[0, owner * 4 + 2 * j + k], 4) for k in range(2)], axis=1)
            lat_low[:, rows] = both.astype(BF16)
            cols = both.T.astype(BF16)
            for t, (base, full, turned) in enumerate(
                ((kb, ka, kt), (vb, va, vt), (qb, qa, None), (dcb, ua, None))
            ):
                kind = (1, 2, 0, 3)[t]
                extra = dot(cols, up_pad[:, WIDTH * kind : WIDTH * (kind + 1)])
                for h in range(4):
                    low = (base[h, rows, :].astype(F32) + extra[:, HD * h : HD * (h + 1)]).astype(BF16)
                    full[h, rows, :] = low
                    if turned is not None:
                        turned[h, :, rows] = low.T

    for copy in loads[25:]:
        copy.wait()
    with jax.named_scope("adapt"):
        adapt(core)
    with jax.named_scope("latent_sum"):
        next(latents)
    for c in range(2):
        send(
            total.at[0, pl.ds(4 * c + 2, 2), pl.ds(RANK, 2 * RANK)], lat_prev.at[pl.ds(2 * c, 2)],
            lp_send.at[c], lp_recv.at[c], {"ctx": after},
        )
    with jax.named_scope("adapt"):
        adapt(1 - core)

    def chunk(j, slot, at, with_off, c, sums):
        h = head_of[slot]
        off = slot if slot < 2 else None
        s, g, p, ds = (ref.at[j % 2] for ref in (score, grad_prob, prob_low, grad_low))
        ahead = HALF if with_off else 0
        length = ahead + CHUNK * (c + 1)
        strips = length // STRIP
        here = slice(at + CHUNK * c, at + CHUNK * (c + 1))
        held = {}

        def key_rows(t, b):
            first = CHUNK * b
            if first >= ahead:
                return (ka, va)[t][h, at + first - ahead : at + first - ahead + CHUNK, :]
            if off is not None:
                return off_rows[off, t, first : first + CHUNK]
            return (ka, va)[t][h, first : first + CHUNK, :]

        def key_cols(t):
            own = (kt, vt)[t][h, :, at : at + length - ahead]
            if not with_off:
                return own
            early = off_cols[off, t] if off is not None else (kt, vt)[t][h, :, :HALF]
            return jnp.concatenate([early, own], axis=1)

        def strip(i):
            return slice(STRIP * i, STRIP * (i + 1))

        def scores_of(b):
            s[CHUNK * b : CHUNK * (b + 1), :] = dot(key_rows(0, b), qa[h, here, :], NT)

        def grad_probs_of(b):
            g[CHUNK * b : CHUNK * (b + 1), :] = dot(key_rows(1, b), ua[h, here, :], NT)

        def causal(i):
            value = s[strip(i), :]
            first = STRIP * i - (length - CHUNK)
            if first < 0:
                return value
            key = lax.broadcasted_iota(jnp.int32, value.shape, 0) + first
            return jnp.where(key <= lax.broadcasted_iota(jnp.int32, value.shape, 1), value, -jnp.inf)

        def peaks(i):
            peak = fold_strip(causal(i), jnp.maximum)
            held["peak"] = peak if i == 0 else jnp.maximum(held["peak"], peak)

        def weigh(i):
            if i == 0:
                held["peak"] = jnp.max(held["peak"], axis=0, keepdims=True)
                held["sum"] = held["center"] = jnp.zeros((8, CHUNK), F32)
            weights = jnp.exp2((causal(i) - held["peak"]) * EXP_SCALE)
            s[strip(i), :] = weights
            held["sum"] = held["sum"] + fold_strip(weights, jnp.add)
            held["center"] = held["center"] + fold_strip(weights * g[strip(i), :], jnp.add)

        def finish(i):
            if i == 0:
                held["inverse"] = 1.0 / jnp.sum(held["sum"], axis=0, keepdims=True)
                held["center"] = jnp.sum(held["center"], axis=0, keepdims=True) * held["inverse"]
                held["scaled"] = held["inverse"] * SCALE
            weights = s[strip(i), :]
            p[strip(i), :] = (weights * held["inverse"]).astype(BF16)
            ds[strip(i), :] = ((weights * held["scaled"]) * (g[strip(i), :] - held["center"])).astype(BF16)

        def query_side():
            grad_q[slot, :, here] = dot(key_cols(0), ds[:length, :]).astype(BF16)

        def context_side():
            ctx_all[slot, :, here] = dot(key_cols(1), p[:length, :]).astype(BF16)

        def key_side(t, b):
            low, rows = ((ds, qa), (p, ua))[t]
            value = dot(low[CHUNK * b : CHUNK * (b + 1), :], rows[h, here, :])
            name = (t, with_off, b)
            sums[name] = sums[name] + value if name in sums else value

        blocks = range(length // CHUNK)
        before_it = [functools.partial(f, b) for b in blocks for f in (scores_of, grad_probs_of)]
        middle = [functools.partial(f, i) for f in (peaks, weigh, finish) for i in range(strips)]
        after_it = [query_side, context_side] + [functools.partial(key_side, t, b) for b in blocks for t in (0, 1)]
        return before_it, middle, after_it

    def keys_done(slot, sums):
        for t, (grad, away) in enumerate(((grad_k, back_k), (grad_v, back_v))):
            for b in range(2):
                early, late = slice(CHUNK * b, CHUNK * (b + 1)), slice(HALF + CHUNK * b, HALF + CHUNK * (b + 1))
                first, off, last = sums[t, False, b], sums[t, True, b], sums[t, True, b + 2]
                if slot < 2:
                    away[slot, early] = off.astype(BF16)
                    grad[slot, early] = last.astype(BF16)
                    grad[slot, late] = first.astype(BF16)
                else:
                    grad[slot, early] = (first + off).astype(BF16)
                    grad[slot, late] = last.astype(BF16)

    def factors(t, slots):
        return jnp.concatenate([fac[t, head_of[slot]] for slot in slots], axis=1)

    def stacked(ref, slots):
        return jnp.concatenate([ref[slot] for slot in slots], axis=0)

    def beside(ref, slots):
        return jnp.concatenate([ref[slot] for slot in slots], axis=1)

    def projections(slots):
        return [
            dot(factors(0, slots), stacked(grad_q, slots)),
            dot(factors(1, slots), beside(grad_k, slots), NT),
            dot(factors(2, slots), beside(grad_v, slots), NT),
            dot(factors(3, slots), stacked(ctx_all, slots)),
        ]

    def back_copy(c):
        return remote(
            back.at[c], back_in.at[core], back_send.at[c], back_recv.at[core],
            {"ctx": before, "head": y * 2 + c},
        )

    def latents_from_before():
        for c in range(2):
            remote(
                total.at[0, pl.ds(4 * c + 2, 2), pl.ds(RANK, 2 * RANK)], lat_prev.at[pl.ds(2 * c, 2)],
                lp_send.at[c], lp_recv.at[c], {"ctx": after},
            ).wait_recv()
        for b in range(4):
            both = split_rows(2.0 * lat_prev[b], 2)
            prev_low[:, HD * b : HD * (b + 1)] = both.astype(BF16)
            prev_cols[HD * b : HD * (b + 1), :] = both.T.astype(BF16)

    def keys_from_before(slot):
        if slot == 0:
            latents_from_before()
        remote(
            kv_stage.at[slot], kv_in.at[slot], kv_send.at[slot], kv_recv.at[slot], {"ctx": after}
        ).wait_recv()
        for t in range(2):
            extra = dot(prev_cols[...], prev_up[t, head_of[slot]])
            low = (kv_in[slot, t].astype(F32) + extra).astype(BF16)
            off_rows[slot, t] = low
            off_cols[slot, t] = low.T

    def send_back():
        for t, ref in ((1, back_k), (2, back_v)):
            value = dot(factors(t, (0, 1)), beside(ref, (0, 1)), NT)
            for b in range(4):
                back[b // 2, b % 2, RANK * (t - 1) : RANK * t] = value[:, HD * b : HD * (b + 1)]
        for c in range(2):
            back_copy(c).start()

    with jax.named_scope("attend"):
        chunks, at_start, at_end, shares = [], {}, {}, []
        all_sums = [{}, {}, {}, {}]
        order = [(0, False), (1, False), (2, False), (2, True), (0, True), (1, True), (3, True), (3, False)]
        for slot, with_off in order:
            first_at = HALF if slot < 2 else 0
            if slot < 2 and with_off:
                at_start[len(chunks)] = functools.partial(keys_from_before, slot)
            for c in ((1, 0) if (slot, with_off) == (3, False) else (0, 1)):
                at = HALF - first_at if with_off else first_at
                chunks.append(chunk(len(chunks), slot, at, with_off, c, all_sums[slot]))
            if with_off != (slot == 3):
                at_end[len(chunks) - 1] = functools.partial(keys_done, slot, all_sums[slot])
        count = len(chunks)
        for step in chunks[0][0]:
            step()
        for j in range(count + 1):
            if j + 1 in at_start:
                at_start[j + 1]()
            lists = [chunks[j][1]] if j < count else []
            lists += [chunks[j + 1][0]] if j + 1 < count else []
            lists += [chunks[j - 1][2]] if j else []
            for step in merged(*lists):
                step()
            if j - 1 in at_end:
                at_end[j - 1]()
            if j - 1 == 11:
                send_back()
            if j == count - 1:
                shares = [a + b for a, b in zip(projections((0, 1)), projections((2,)))]
        wide = jnp.concatenate([a + b for a, b in zip(shares, projections((3,)))], axis=0)

    with jax.named_scope("share_sum"):
        for b in range(8):
            part[1, place(b)] = wide[:, HD * b : HD * (b + 1)]

        def add_back():
            for c in range(2):
                remote(back.at[c], back_in.at[c], back_send.at[c], back_recv.at[c], sibling).wait_recv()
            none = jnp.zeros((RANK, HD), F32)
            return [0.0, 0.0] + [
                jnp.concatenate([none, back_in[0, i] + back_in[1, i], none], axis=0) for i in range(2)
            ]

        shares = sum_heads(1, add_back)
        next(shares)
        every = (0, 1, 2, 3)
        up_rows = [
            None,
            fold(dot(lat_low[32:64, :], beside(grad_k, every))),
            fold(dot(lat_low[64:96, :], beside(grad_v, every))),
            None,
        ]
        next(shares)
        up_rows[0] = fold(dot(lat_low[:32, :], stacked(grad_q, every), NT))
        up_rows[3] = fold(dot(lat_low[96:, :], stacked(ctx_all, every), NT))
        for t, ref in ((1, back_k), (2, back_v)):
            extra = fold(dot(prev_low[32 * t - 32 : 32 * t, :], beside(ref, (0, 1))))
            up_rows[t] = up_rows[t] + jnp.concatenate([extra, jnp.zeros_like(extra)], axis=1)
        up_rows = jnp.concatenate(up_rows, axis=0)
        for slot in every:
            up_sum[slot] = up_rows[:, HD * slot : HD * (slot + 1)]
        for h in range(4):
            cut[0, h] = up_sum[jnp.minimum(slot_of[h], 3)].astype(BF16)
        ups = sum_tokens(0)
        next(ups)
        next(shares)
        next(ups)

    def down_gradients(owner):
        wide = jnp.concatenate([split_rows(2.0 * total[1, owner * 4 + i], 4).astype(BF16) for i in range(4)], axis=1)
        down = jnp.zeros((96, WIDTH), F32)
        last = jnp.zeros((32, WIDTH), F32)
        for j in range(2):
            rows = rows_of(owner, j)
            here = wide[:, 256 * j : 256 * (j + 1)]
            down = down + dot(here[:96], xb[rows, :])
            last = last + dot(here[96:], dob[rows, :])
        return jnp.concatenate([fold(down[32 * t : 32 * t + 32]) for t in range(3)] + [fold(last)], axis=0)

    with jax.named_scope("down_gradients"):
        down = down_gradients(core)
        next(shares)
        down = down + down_gradients(1 - core)
        for c in range(4):
            cut[1, c] = down[:, HD * c : HD * (c + 1)].astype(BF16)
    with jax.named_scope("token_sum"):
        downs = sum_tokens(1)
        next(downs)
        next(downs)
        next(ups)
        next(downs)
        next(ups)
        next(downs)
    for copy in sends:
        copy.wait_send()
    for c in range(2):
        back_copy(c).wait_send()


def on_device(
    inputs, q_base, k_base, v_base, d_out, d_ctx_base, flags,
    query_down_factor, up_q, key_down_factor, up_k, value_down_factor, up_v, down_o, output_up_factor,
):
    anywhere = pl.BlockSpec(memory_space=pl.ANY)
    vmem = pl.BlockSpec(memory_space=pltpu.VMEM)
    dma = pltpu.SemaphoreType.DMA
    v = pltpu.VMEM
    out = pl.pallas_call(
        kernel,
        out_shape=pltpu.VMEM((2, 64, WIDTH), F32),
        in_specs=[anywhere] * 15,
        out_specs=vmem,
        scratch_shapes=[
            pltpu.SMEM((4,), jnp.int32), v((4, RANK, WIDTH), BF16), v((4, RANK, WIDTH), BF16),
            v((ROWS, WIDTH), BF16), *[v((4, ROWS, HD), BF16) for _ in range(3)],
            v((ROWS, WIDTH), BF16), v((4, ROWS, HD), BF16),
            v((2, 2, HALF, HD), BF16), v((2, 2, HALF, HD), BF16),
            v((2, 8, 64, HD), F32), v((2, 4, 64, HD), F32), v((2, 4, 64, HD), BF16),
            v((2, 3, 4, 64, HD), BF16), v((2, 8, 64, HD), F32),
            v((4, 32, HD), F32), v((128, 4 * WIDTH), BF16), v((4, 4, RANK, HD), BF16),
            v((2, 4, 64, HD), BF16), v((128, ROWS), BF16),
            v((64, HALF), BF16), v((HALF, 64), BF16),
            *[v((4, ROWS, HD), BF16) for _ in range(4)],
            *[v((4, HD, ROWS), BF16) for _ in range(2)],
            v((4, HD, ROWS), BF16), v((4, ROWS, HD), BF16), v((4, ROWS, HD), BF16), v((4, HD, ROWS), BF16),
            v((2, HALF, HD), BF16), v((2, HALF, HD), BF16), v((2, 2, HALF, HD), BF16), v((2, 2, HD, HALF), BF16),
            v((2, ROWS, CHUNK), F32), v((2, ROWS, CHUNK), F32), v((2, ROWS, CHUNK), BF16), v((2, ROWS, CHUNK), BF16),
            v((2, 2, 32, HD), F32), v((2, 2, 32, HD), F32), v((4, 64, HD), F32),
            v((2, 4, 64, HD), BF16), v((2, 3, 64, HD), BF16), v((2, 64, HD), BF16),
            v((2, 7, 64, HD), BF16), v((2, 64, HD), BF16), v((2, 4, 64, HD), BF16),
            dma((33,)), dma((2,)), dma((2,)), dma((2,)), dma((2,)), dma((2,)), dma((2,)),
            dma((2,)), dma((2,)), dma((2, 3)), dma((2, 3)), dma((2,)), dma((2,)),
            dma((2, 3)), dma((2, 3)), dma((2, 7)), dma((2, 7)), dma((2, 3)), dma((2, 3)),
        ],
        compiler_params=pltpu.CompilerParams(
            collective_id=0, has_side_effects=True, vmem_limit_bytes=56 * 1024 * 1024
        ),
    )(
        inputs[0], q_base[0], k_base[0], v_base[0], d_out[0], d_ctx_base[0], flags,
        query_down_factor, up_q, key_down_factor, up_k, value_down_factor, up_v, down_o, output_up_factor,
    )
    result = []
    for t in range(4):
        rows = slice(RANK * t, RANK * (t + 1))
        result += [out[1, rows], out[0, rows]]
    return (result[0], result[1], result[2], result[3], result[4], result[5], result[7], result[6])


def solution(mesh):
    tokens = P("dp", "ctx", "head")
    factor = P(None, "head")
    return jax.shard_map(
        on_device,
        mesh=mesh,
        in_specs=(tokens,) * 6 + (P("head"),) + (factor,) * 8,
        out_specs=(factor,) * 8,
        check_vma=False,
    )
```

```python
import functools
import math

import jax
import jax.numpy as jnp
from jax import lax
from jax.experimental import pallas as pl
from jax.experimental.pallas import tpu as pltpu
from jax.sharding import PartitionSpec as P

HD = 128
ROWS = 1024
HALF = 512
CHUNK = 256
STRIP = 64
RANK = 16
WIDTH = 512
NY, NZ, NX = 4, 8, 4
Y_ORDER = X_ORDER = (2, 1, 3)
Z_ORDER = (4, 3, 5, 2, 6, 1, 7)
SCALE = 1.0 / math.sqrt(HD)
EXP_SCALE = SCALE * math.log2(math.e)
MESH = pl.DeviceIdType.MESH
F32 = jnp.float32
BF16 = jnp.bfloat16
NN = (((1,), (0,)), ((), ()))
NT = (((1,), (1,)), ((), ()))


def dot(a, b, dims=NN):
    return lax.dot_general(a, b, dims, preferred_element_type=F32)


def place(block):
    return (block // 2) % 2 * 4 + block % 2 + 2 * (block // 4)


def split_rows(wide, kinds):
    rows = []
    for t in range(kinds):
        part = wide[RANK * t : RANK * (t + 1)]
        high = part.astype(BF16).astype(F32)
        rows += [high, part - high]
    return jnp.concatenate(rows, axis=0)


def fold(pair):
    return pair[:RANK] + pair[RANK:]


def fold_strip(strip, op):
    strip = strip.reshape(STRIP // 8, 8, CHUNK)
    result = strip[0]
    for i in range(1, STRIP // 8):
        result = op(result, strip[i])
    return result


def merged(*lists):
    timed = [((i + 0.5) / len(steps), k, step) for k, steps in enumerate(lists) for i, step in enumerate(steps)]
    return [step for _, _, step in sorted(timed, key=lambda item: item[:2])]


def kernel(
    x_hbm, q_hbm, k_hbm, v_hbm, do_hbm, dc_hbm, flags_hbm,
    down_q_hbm, up_q_hbm, down_k_hbm, up_k_hbm, down_v_hbm, up_v_hbm, down_o_hbm, up_o_hbm,
    out_ref,
    flags, firsts, seconds,
    xb, qb, kb, vb, dob, dcb,
    kv_stage, kv_in,
    part, sib_in, acc, y_in, total,
    lat_prev, up_pad, fac, prev_up, lat_low, prev_low, prev_cols,
    qa, ka, va, ua, kt, vt,
    grad_q, grad_k, grad_v, ctx_all, back_k, back_v, off_rows, off_cols,
    score, grad_prob, prob_low, grad_low,
    back, back_in, up_sum,
    cut, x_in, x_sum, z_in, z_all, x_all,
    load_sem, kv_send, kv_recv, lp_send, lp_recv, back_send, back_recv,
    sib_send, sib_recv, y_send, y_recv, fw_send, fw_recv,
    x1_send, x1_recv, z_send, z_recv, x2_send, x2_recv,
):
    ctx, head, dp = lax.axis_index("ctx"), lax.axis_index("head"), lax.axis_index("dp")
    y, core = head // 2, head % 2
    x_lo, z = ctx // NZ, ctx % NZ
    x = dp * 2 + x_lo
    sibling = {"head": y * 2 + (1 - core)}
    after = lax.rem(ctx + 1, 2 * NZ)
    before = lax.rem(ctx + 2 * NZ - 1, 2 * NZ)

    def y_peer(d):
        return {"head": lax.rem(y + d, NY) * 2 + core}

    def z_peer(d):
        return {"ctx": x_lo * NZ + lax.rem(z + d, NZ)}

    def x_peer(d):
        other = lax.rem(x + d, NX)
        return {"ctx": (other % 2) * NZ + z, "dp": other // 2}

    loads = []

    def load(*pairs):
        for source, target in pairs:
            copy = pltpu.make_async_copy(source, target, load_sem.at[len(loads)])
            copy.start()
            loads.append(copy)

    def by_head(source, target):
        return [(source.at[:, pl.ds(HD * h, HD)], target.at[h]) for h in range(4)]

    def rows_of(owner, j):
        return pl.ds(pl.multiple_of(owner * 256 + HALF * j, 256), 256)

    def by_owner(owner):
        rows = [rows_of(owner, j) for j in range(2)]
        return [(source.at[r], target.at[r]) for source, target in ((x_hbm, xb), (do_hbm, dob)) for r in rows]

    load(
        (down_q_hbm, firsts.at[0]), (down_k_hbm, firsts.at[1]), (down_v_hbm, firsts.at[2]), (up_o_hbm, firsts.at[3]),
        *by_owner(1 - core), *by_owner(core), (flags_hbm, flags), *by_head(k_hbm, kb), *by_head(v_hbm, vb),
    )

    barrier = pltpu.get_barrier_semaphore()
    peers = [sibling]
    peers += [y_peer(d) for d in range(1, NY)]
    peers += [z_peer(d) for d in range(1, NZ)]
    peers += [x_peer(d) for d in range(1, NX)]
    for near in (after, before):
        peers += [{"ctx": near}, {"ctx": near, "head": y * 2 + (1 - core)}]
    for peer in peers:
        pl.semaphore_signal(barrier, inc=1, device_id=peer, device_id_type=MESH)

    sends = []

    def remote(source, target, send_sem, recv_sem, peer):
        return pltpu.make_async_remote_copy(
            src_ref=source, dst_ref=target, send_sem=send_sem, recv_sem=recv_sem,
            device_id=peer, device_id_type=MESH,
        )

    def send(*args):
        copy = remote(*args)
        copy.start()
        sends.append(copy)

    def own_latents(owner):
        first = firsts[...].reshape(4 * RANK, WIDTH)
        for j in range(2):
            rows = rows_of(owner, j)
            lat_part = dot(first[: 3 * RANK], xb[rows, :], NT)
            mix_part = dot(first[3 * RANK :], dob[rows, :], NT)
            for k in range(2):
                part[0, owner * 4 + 2 * j + k, : 3 * RANK] = lat_part[:, HD * k : HD * (k + 1)]
                part[0, owner * 4 + 2 * j + k, 3 * RANK :] = mix_part[:, HD * k : HD * (k + 1)]

    for copy in loads[:8]:
        copy.wait()
    with jax.named_scope("own_latents"):
        own_latents(1 - core)
    with jax.named_scope("entry_barrier"):
        pl.semaphore_wait(barrier, len(peers))

    mine = core * 4
    other = (1 - core) * 4

    def sum_heads(p, late=None):
        pair = (part.at[p, pl.ds(other, 4)], sib_in.at[p], sib_send.at[p], sib_recv.at[p], sibling)
        send(*pair)
        yield
        remote(*pair).wait_recv()
        extra = [0.0] * 4 if late is None else late()
        for i in range(4):
            acc[p, i] = (part[p, mine + i] + sib_in[p, i] + extra[i]).astype(BF16)
        shares = [(acc.at[p], y_in.at[p, d - 1], y_send.at[p, d - 1], y_recv.at[p, d - 1], y_peer(d)) for d in Y_ORDER]
        for share in shares:
            send(*share)
        yield
        for share in shares:
            remote(*share).wait_recv()
        for i in range(4):
            summed = acc[p, i].astype(F32)
            for d in range(1, NY):
                summed = summed + y_in[p, d - 1, i].astype(F32)
            total[p, mine + i] = summed
        own = total.at[p, pl.ds(mine, 4)]
        send(own, own, fw_send.at[p], fw_recv.at[p], sibling)
        yield
        came = total.at[p, pl.ds(other, 4)]
        remote(came, came, fw_send.at[p], fw_recv.at[p], sibling).wait_recv()
        yield

    def sum_tokens(e):
        for d in X_ORDER:
            send(cut.at[e, lax.rem(x + d, NX)], x_in.at[e, d - 1], x1_send.at[e, d - 1], x1_recv.at[e, d - 1], x_peer(d))
        yield
        summed = cut[e, x].astype(F32)
        for d in range(1, NX):
            remote(cut.at[e, 0], x_in.at[e, d - 1], x1_send.at[e, d - 1], x1_recv.at[e, d - 1], x_peer(d)).wait_recv()
            summed = summed + x_in[e, d - 1].astype(F32)
        x_sum[e] = summed.astype(BF16)
        shares = [(x_sum.at[e], z_in.at[e, d - 1], z_send.at[e, d - 1], z_recv.at[e, d - 1], z_peer(d)) for d in Z_ORDER]
        for share in shares:
            send(*share)
        yield
        summed = x_sum[e].astype(F32)
        for share in shares:
            remote(*share).wait_recv()
        for d in range(1, NZ):
            summed = summed + z_in[e, d - 1].astype(F32)
        z_all[e] = summed.astype(BF16)
        for d in X_ORDER:
            send(z_all.at[e], x_all.at[e, x], x2_send.at[e, d - 1], x2_recv.at[e, d - 1], x_peer(d))
        x_all[e, x] = z_all[e]
        yield
        for d in range(1, NX):
            came = x_all.at[e, lax.rem(x + NX - d, NX)]
            remote(z_all.at[e], came, x2_send.at[e, d - 1], x2_recv.at[e, d - 1], x_peer(d)).wait_recv()
        for c in range(4):
            out_ref[e, :, HD * c : HD * (c + 1)] = x_all[e, c].astype(F32)
        yield

    latents = sum_heads(0)
    next(latents)
    load(
        (up_q_hbm, seconds.at[0]), (up_k_hbm, seconds.at[1]), (up_v_hbm, seconds.at[2]), (down_o_hbm, seconds.at[3]),
    )
    for copy in loads[8:13]:
        copy.wait()
    with jax.named_scope("own_latents"):
        own_latents(core)

    f0, f1, f2, f3 = (flags[h] for h in range(4))
    head_of = (
        (1 - f0) * (2 - f1),
        3 * f3 + (1 - f3) * (1 + f2),
        f0 * (1 + f1),
        3 * (1 - f3) + f3 * (2 - f2),
    )
    slot_of = (
        2 - 2 * f0,
        f1 * f0 + (1 - f1) * (2 + 1 - f0),
        f2 * (f0 + f1) + (1 - f2) * (4 - f0 - f1),
        f3 + (1 - f3) * 3,
    )

    def stage_keys(slot):
        for i, base in enumerate((kb, vb)):
            kv_stage[slot, i] = base[head_of[slot], HALF:, :]
        send(kv_stage.at[slot], kv_in.at[slot], kv_send.at[slot], kv_recv.at[slot], {"ctx": after})

    for copy in loads[13:21]:
        copy.wait()
    with jax.named_scope("stage_keys"):
        stage_keys(0)
    with jax.named_scope("latent_sum"):
        next(latents)

    load(*by_head(q_hbm, qb), *by_head(dc_hbm, dcb))
    for copy in loads[21:25]:
        copy.wait()
    up_pad[...] = jnp.zeros_like(up_pad)
    for t, factor in enumerate(seconds[t] for t in range(4)):
        for copy_at in (0, RANK):
            up_pad[32 * t + copy_at : 32 * t + copy_at + RANK, WIDTH * t : WIDTH * (t + 1)] = factor
        for h in range(4):
            fac[t, h] = factor[:, HD * h : HD * (h + 1)]
    for t in range(2):
        for h in range(4):
            at = WIDTH * (1 + t) + HD * h
            prev_up[t, h] = up_pad[32:96, at : at + HD]

    with jax.named_scope("latent_sum"):
        next(latents)

    def adapt(owner):
        for j in range(2):
            rows = rows_of(owner, j)
            both = jnp.concatenate([split_rows(2.0 * total[0, owner * 4 + 2 * j + k], 4) for k in range(2)], axis=1)
            lat_low[:, rows] = both.astype(BF16)
            cols = both.T.astype(BF16)
            for t, (base, full, turned) in enumerate(
                ((kb, ka, kt), (vb, va, vt), (qb, qa, None), (dcb, ua, None))
            ):
                kind = (1, 2, 0, 3)[t]
                extra = dot(cols, up_pad[:, WIDTH * kind : WIDTH * (kind + 1)])
                for h in range(4):
                    low = (base[h, rows, :].astype(F32) + extra[:, HD * h : HD * (h + 1)]).astype(BF16)
                    full[h, rows, :] = low
                    if turned is not None:
                        turned[h, :, rows] = low.T

    for copy in loads[25:]:
        copy.wait()
    with jax.named_scope("adapt"):
        adapt(core)
    with jax.named_scope("latent_sum"):
        next(latents)
    for c in range(2):
        send(
            total.at[0, pl.ds(4 * c + 2, 2), pl.ds(RANK, 2 * RANK)], lat_prev.at[pl.ds(2 * c, 2)],
            lp_send.at[c], lp_recv.at[c], {"ctx": after},
        )
    with jax.named_scope("stage_keys"):
        stage_keys(1)
    with jax.named_scope("adapt"):
        adapt(1 - core)

    def chunk(j, slot, at, with_off, c, sums):
        h = head_of[slot]
        off = slot if slot < 2 else None
        s, g, p, ds = (ref.at[j % 2] for ref in (score, grad_prob, prob_low, grad_low))
        ahead = HALF if with_off else 0
        length = ahead + CHUNK * (c + 1)
        strips = length // STRIP
        here = slice(at + CHUNK * c, at + CHUNK * (c + 1))
        held = {}

        def key_rows(t, b):
            first = CHUNK * b
            if first >= ahead:
                return (ka, va)[t][h, at + first - ahead : at + first - ahead + CHUNK, :]
            if off is not None:
                return off_rows[off, t, first : first + CHUNK]
            return (ka, va)[t][h, first : first + CHUNK, :]

        def key_cols(t):
            own = (kt, vt)[t][h, :, at : at + length - ahead]
            if not with_off:
                return own
            early = off_cols[off, t] if off is not None else (kt, vt)[t][h, :, :HALF]
            return jnp.concatenate([early, own], axis=1)

        def strip(i):
            return slice(STRIP * i, STRIP * (i + 1))

        def scores_of(b):
            s[CHUNK * b : CHUNK * (b + 1), :] = dot(key_rows(0, b), qa[h, here, :], NT)

        def grad_probs_of(b):
            g[CHUNK * b : CHUNK * (b + 1), :] = dot(key_rows(1, b), ua[h, here, :], NT)

        def causal(i):
            value = s[strip(i), :]
            first = STRIP * i - (length - CHUNK)
            if first < 0:
                return value
            key = lax.broadcasted_iota(jnp.int32, value.shape, 0) + first
            return jnp.where(key <= lax.broadcasted_iota(jnp.int32, value.shape, 1), value, -jnp.inf)

        def peaks(i):
            peak = fold_strip(causal(i), jnp.maximum)
            held["peak"] = peak if i == 0 else jnp.maximum(held["peak"], peak)

        def weigh(i):
            if i == 0:
                held["peak"] = jnp.max(held["peak"], axis=0, keepdims=True)
                held["sum"] = held["center"] = jnp.zeros((8, CHUNK), F32)
            weights = jnp.exp2((causal(i) - held["peak"]) * EXP_SCALE)
            s[strip(i), :] = weights
            held["sum"] = held["sum"] + fold_strip(weights, jnp.add)
            held["center"] = held["center"] + fold_strip(weights * g[strip(i), :], jnp.add)

        def finish(i):
            if i == 0:
                held["inverse"] = 1.0 / jnp.sum(held["sum"], axis=0, keepdims=True)
                held["center"] = jnp.sum(held["center"], axis=0, keepdims=True) * held["inverse"]
                held["scaled"] = held["inverse"] * SCALE
            weights = s[strip(i), :]
            p[strip(i), :] = (weights * held["inverse"]).astype(BF16)
            ds[strip(i), :] = ((weights * held["scaled"]) * (g[strip(i), :] - held["center"])).astype(BF16)

        def query_side():
            grad_q[slot, :, here] = dot(key_cols(0), ds[:length, :]).astype(BF16)

        def context_side():
            ctx_all[slot, :, here] = dot(key_cols(1), p[:length, :]).astype(BF16)

        def key_side(t, b):
            low, rows = ((ds, qa), (p, ua))[t]
            value = dot(low[CHUNK * b : CHUNK * (b + 1), :], rows[h, here, :])
            name = (t, with_off, b)
            sums[name] = sums[name] + value if name in sums else value

        blocks = range(length // CHUNK)
        before_it = [functools.partial(f, b) for b in blocks for f in (scores_of, grad_probs_of)]
        middle = [functools.partial(f, i) for f in (peaks, weigh, finish) for i in range(strips)]
        after_it = [query_side, context_side] + [functools.partial(key_side, t, b) for b in blocks for t in (0, 1)]
        return before_it, middle, after_it

    def keys_done(slot, sums):
        for t, (grad, away) in enumerate(((grad_k, back_k), (grad_v, back_v))):
            for b in range(2):
                early, late = slice(CHUNK * b, CHUNK * (b + 1)), slice(HALF + CHUNK * b, HALF + CHUNK * (b + 1))
                first, off, last = sums[t, False, b], sums[t, True, b], sums[t, True, b + 2]
                if slot < 2:
                    away[slot, early] = off.astype(BF16)
                    grad[slot, early] = last.astype(BF16)
                    grad[slot, late] = first.astype(BF16)
                else:
                    grad[slot, early] = (first + off).astype(BF16)
                    grad[slot, late] = last.astype(BF16)

    def factors(t, slots):
        return jnp.concatenate([fac[t, head_of[slot]] for slot in slots], axis=1)

    def stacked(ref, slots):
        return jnp.concatenate([ref[slot] for slot in slots], axis=0)

    def beside(ref, slots):
        return jnp.concatenate([ref[slot] for slot in slots], axis=1)

    def projections(slots):
        return [
            dot(factors(0, slots), stacked(grad_q, slots)),
            dot(factors(1, slots), beside(grad_k, slots), NT),
            dot(factors(2, slots), beside(grad_v, slots), NT),
            dot(factors(3, slots), stacked(ctx_all, slots)),
        ]

    def back_copy(c):
        return remote(
            back.at[c], back_in.at[core], back_send.at[c], back_recv.at[core],
            {"ctx": before, "head": y * 2 + c},
        )

    def latents_from_before():
        for c in range(2):
            remote(
                total.at[0, pl.ds(4 * c + 2, 2), pl.ds(RANK, 2 * RANK)], lat_prev.at[pl.ds(2 * c, 2)],
                lp_send.at[c], lp_recv.at[c], {"ctx": after},
            ).wait_recv()
        for b in range(4):
            both = split_rows(2.0 * lat_prev[b], 2)
            prev_low[:, HD * b : HD * (b + 1)] = both.astype(BF16)
            prev_cols[HD * b : HD * (b + 1), :] = both.T.astype(BF16)

    def keys_from_before(slot):
        if slot == 0:
            latents_from_before()
        remote(
            kv_stage.at[slot], kv_in.at[slot], kv_send.at[slot], kv_recv.at[slot], {"ctx": after}
        ).wait_recv()
        for t in range(2):
            extra = dot(prev_cols[...], prev_up[t, head_of[slot]])
            low = (kv_in[slot, t].astype(F32) + extra).astype(BF16)
            off_rows[slot, t] = low
            off_cols[slot, t] = low.T

    def send_back():
        for t, ref in ((1, back_k), (2, back_v)):
            value = dot(factors(t, (0, 1)), beside(ref, (0, 1)), NT)
            for b in range(4):
                back[b // 2, b % 2, RANK * (t - 1) : RANK * t] = value[:, HD * b : HD * (b + 1)]
        for c in range(2):
            back_copy(c).start()

    with jax.named_scope("attend"):
        chunks, at_start, at_end, shares = [], {}, {}, []
        all_sums = [{}, {}, {}, {}]
        order = [(0, False), (1, False), (2, False), (2, True), (0, True), (3, True), (1, True), (3, False)]
        for slot, with_off in order:
            first_at = HALF if slot < 2 else 0
            if slot < 2 and with_off:
                at_start[len(chunks)] = functools.partial(keys_from_before, slot)
            for c in ((1, 0) if (slot, with_off) == (3, False) else (0, 1)):
                at = HALF - first_at if with_off else first_at
                chunks.append(chunk(len(chunks), slot, at, with_off, c, all_sums[slot]))
            if with_off != (slot == 3):
                at_end[len(chunks) - 1] = functools.partial(keys_done, slot, all_sums[slot])
        count = len(chunks)
        for step in chunks[0][0]:
            step()
        for j in range(count + 1):
            if j + 1 in at_start:
                at_start[j + 1]()
            lists = [chunks[j][1]] if j < count else []
            lists += [chunks[j + 1][0]] if j + 1 < count else []
            lists += [chunks[j - 1][2]] if j else []
            for step in merged(*lists):
                step()
            if j - 1 in at_end:
                at_end[j - 1]()
            if j - 1 == 13:
                send_back()
            if j == count - 1:
                shares = [a + b for a, b in zip(projections((0, 1)), projections((2,)))]
        wide = jnp.concatenate([a + b for a, b in zip(shares, projections((3,)))], axis=0)

    with jax.named_scope("share_sum"):
        for b in range(8):
            part[1, place(b)] = wide[:, HD * b : HD * (b + 1)]

        def add_back():
            for c in range(2):
                remote(back.at[c], back_in.at[c], back_send.at[c], back_recv.at[c], sibling).wait_recv()
            none = jnp.zeros((RANK, HD), F32)
            return [0.0, 0.0] + [
                jnp.concatenate([none, back_in[0, i] + back_in[1, i], none], axis=0) for i in range(2)
            ]

        shares = sum_heads(1, add_back)
        next(shares)
        every = (0, 1, 2, 3)
        up_rows = [
            None,
            fold(dot(lat_low[32:64, :], beside(grad_k, every))),
            fold(dot(lat_low[64:96, :], beside(grad_v, every))),
            None,
        ]
        next(shares)
        up_rows[0] = fold(dot(lat_low[:32, :], stacked(grad_q, every), NT))
        up_rows[3] = fold(dot(lat_low[96:, :], stacked(ctx_all, every), NT))
        for t, ref in ((1, back_k), (2, back_v)):
            extra = fold(dot(prev_low[32 * t - 32 : 32 * t, :], beside(ref, (0, 1))))
            up_rows[t] = up_rows[t] + jnp.concatenate([extra, jnp.zeros_like(extra)], axis=1)
        up_rows = jnp.concatenate(up_rows, axis=0)
        for slot in every:
            up_sum[slot] = up_rows[:, HD * slot : HD * (slot + 1)]
        for h in range(4):
            cut[0, h] = up_sum[jnp.minimum(slot_of[h], 3)].astype(BF16)
        ups = sum_tokens(0)
        next(ups)
        next(shares)
        next(ups)

    def down_gradients(owner):
        wide = jnp.concatenate([split_rows(2.0 * total[1, owner * 4 + i], 4).astype(BF16) for i in range(4)], axis=1)
        down = jnp.zeros((96, WIDTH), F32)
        last = jnp.zeros((32, WIDTH), F32)
        for j in range(2):
            rows = rows_of(owner, j)
            here = wide[:, 256 * j : 256 * (j + 1)]
            down = down + dot(here[:96], xb[rows, :])
            last = last + dot(here[96:], dob[rows, :])
        return jnp.concatenate([fold(down[32 * t : 32 * t + 32]) for t in range(3)] + [fold(last)], axis=0)

    with jax.named_scope("down_gradients"):
        down = down_gradients(core)
        next(shares)
        down = down + down_gradients(1 - core)
        for c in range(4):
            cut[1, c] = down[:, HD * c : HD * (c + 1)].astype(BF16)
    with jax.named_scope("token_sum"):
        downs = sum_tokens(1)
        next(downs)
        next(downs)
        next(ups)
        next(downs)
        next(ups)
        next(downs)
    for copy in sends:
        copy.wait_send()
    for c in range(2):
        back_copy(c).wait_send()


def on_device(
    inputs, q_base, k_base, v_base, d_out, d_ctx_base, flags,
    query_down_factor, up_q, key_down_factor, up_k, value_down_factor, up_v, down_o, output_up_factor,
):
    anywhere = pl.BlockSpec(memory_space=pl.ANY)
    vmem = pl.BlockSpec(memory_space=pltpu.VMEM)
    dma = pltpu.SemaphoreType.DMA
    v = pltpu.VMEM
    out = pl.pallas_call(
        kernel,
        out_shape=pltpu.VMEM((2, 64, WIDTH), F32),
        in_specs=[anywhere] * 15,
        out_specs=vmem,
        scratch_shapes=[
            pltpu.SMEM((4,), jnp.int32), v((4, RANK, WIDTH), BF16), v((4, RANK, WIDTH), BF16),
            v((ROWS, WIDTH), BF16), *[v((4, ROWS, HD), BF16) for _ in range(3)],
            v((ROWS, WIDTH), BF16), v((4, ROWS, HD), BF16),
            v((2, 2, HALF, HD), BF16), v((2, 2, HALF, HD), BF16),
            v((2, 8, 64, HD), F32), v((2, 4, 64, HD), F32), v((2, 4, 64, HD), BF16),
            v((2, 3, 4, 64, HD), BF16), v((2, 8, 64, HD), F32),
            v((4, 32, HD), F32), v((128, 4 * WIDTH), BF16), v((4, 4, RANK, HD), BF16),
            v((2, 4, 64, HD), BF16), v((128, ROWS), BF16),
            v((64, HALF), BF16), v((HALF, 64), BF16),
            *[v((4, ROWS, HD), BF16) for _ in range(4)],
            *[v((4, HD, ROWS), BF16) for _ in range(2)],
            v((4, HD, ROWS), BF16), v((4, ROWS, HD), BF16), v((4, ROWS, HD), BF16), v((4, HD, ROWS), BF16),
            v((2, HALF, HD), BF16), v((2, HALF, HD), BF16), v((2, 2, HALF, HD), BF16), v((2, 2, HD, HALF), BF16),
            v((2, ROWS, CHUNK), F32), v((2, ROWS, CHUNK), F32), v((2, ROWS, CHUNK), BF16), v((2, ROWS, CHUNK), BF16),
            v((2, 2, 32, HD), F32), v((2, 2, 32, HD), F32), v((4, 64, HD), F32),
            v((2, 4, 64, HD), BF16), v((2, 3, 64, HD), BF16), v((2, 64, HD), BF16),
            v((2, 7, 64, HD), BF16), v((2, 64, HD), BF16), v((2, 4, 64, HD), BF16),
            dma((33,)), dma((2,)), dma((2,)), dma((2,)), dma((2,)), dma((2,)), dma((2,)),
            dma((2,)), dma((2,)), dma((2, 3)), dma((2, 3)), dma((2,)), dma((2,)),
            dma((2, 3)), dma((2, 3)), dma((2, 7)), dma((2, 7)), dma((2, 3)), dma((2, 3)),
        ],
        compiler_params=pltpu.CompilerParams(
            collective_id=0, has_side_effects=True, vmem_limit_bytes=56 * 1024 * 1024
        ),
    )(
        inputs[0], q_base[0], k_base[0], v_base[0], d_out[0], d_ctx_base[0], flags,
        query_down_factor, up_q, key_down_factor, up_k, value_down_factor, up_v, down_o, output_up_factor,
    )
    result = []
    for t in range(4):
        rows = slice(RANK * t, RANK * (t + 1))
        result += [out[1, rows], out[0, rows]]
    return (result[0], result[1], result[2], result[3], result[4], result[5], result[7], result[6])


def solution(mesh):
    tokens = P("dp", "ctx", "head")
    factor = P(None, "head")
    return jax.shard_map(
        on_device,
        mesh=mesh,
        in_specs=(tokens,) * 6 + (P("head"),) + (factor,) * 8,
        out_specs=(factor,) * 8,
        check_vma=False,
    )
```

```python
import functools
import math

import jax
import jax.numpy as jnp
from jax import lax
from jax.experimental import pallas as pl
from jax.experimental.pallas import tpu as pltpu
from jax.sharding import PartitionSpec as P

HD = 128
ROWS = 1024
HALF = 512
CHUNK = 256
STRIP = 64
RANK = 16
WIDTH = 512
NY, NZ, NX = 4, 8, 4
Y_ORDER = X_ORDER = (2, 1, 3)
Z_ORDER = (4, 3, 5, 2, 6, 1, 7)
SCALE = 1.0 / math.sqrt(HD)
EXP_SCALE = SCALE * math.log2(math.e)
MESH = pl.DeviceIdType.MESH
F32 = jnp.float32
BF16 = jnp.bfloat16
NN = (((1,), (0,)), ((), ()))
NT = (((1,), (1,)), ((), ()))


def dot(a, b, dims=NN):
    return lax.dot_general(a, b, dims, preferred_element_type=F32)


def place(block):
    return (block // 2) % 2 * 4 + block % 2 + 2 * (block // 4)


def split_rows(wide, kinds):
    rows = []
    for t in range(kinds):
        part = wide[RANK * t : RANK * (t + 1)]
        high = part.astype(BF16).astype(F32)
        rows += [high, part - high]
    return jnp.concatenate(rows, axis=0)


def fold(pair):
    return pair[:RANK] + pair[RANK:]


def fold_strip(strip, op):
    strip = strip.reshape(STRIP // 8, 8, CHUNK)
    result = strip[0]
    for i in range(1, STRIP // 8):
        result = op(result, strip[i])
    return result


def merged(*lists):
    timed = [((i + 0.5) / len(steps), k, step) for k, steps in enumerate(lists) for i, step in enumerate(steps)]
    return [step for _, _, step in sorted(timed, key=lambda item: item[:2])]


def kernel(
    x_hbm, q_hbm, k_hbm, v_hbm, do_hbm, dc_hbm, flags_hbm,
    down_q_hbm, up_q_hbm, down_k_hbm, up_k_hbm, down_v_hbm, up_v_hbm, down_o_hbm, up_o_hbm,
    out_ref,
    flags, firsts, seconds,
    xb, qb, kb, vb, dob, dcb,
    kv_stage, kv_in,
    part, sib_in, acc, y_in, total,
    lat_prev, up_pad, fac, prev_up, lat_low, prev_low, prev_cols,
    qa, ka, va, ua, kt, vt,
    grad_q, grad_k, grad_v, ctx_all, back_k, back_v, off_rows, off_cols,
    score, grad_prob, prob_low, grad_low,
    back, back_in, up_sum,
    cut, x_in, x_sum, z_in, z_all, x_all,
    load_sem, kv_send, kv_recv, lp_send, lp_recv, back_send, back_recv,
    sib_send, sib_recv, y_send, y_recv, fw_send, fw_recv,
    x1_send, x1_recv, z_send, z_recv, x2_send, x2_recv,
):
    ctx, head, dp = lax.axis_index("ctx"), lax.axis_index("head"), lax.axis_index("dp")
    y, core = head // 2, head % 2
    x_lo, z = ctx // NZ, ctx % NZ
    x = dp * 2 + x_lo
    sibling = {"head": y * 2 + (1 - core)}
    after = lax.rem(ctx + 1, 2 * NZ)
    before = lax.rem(ctx + 2 * NZ - 1, 2 * NZ)

    def y_peer(d):
        return {"head": lax.rem(y + d, NY) * 2 + core}

    def z_peer(d):
        return {"ctx": x_lo * NZ + lax.rem(z + d, NZ)}

    def x_peer(d):
        other = lax.rem(x + d, NX)
        return {"ctx": (other % 2) * NZ + z, "dp": other // 2}

    loads = []

    def load(*pairs):
        for source, target in pairs:
            copy = pltpu.make_async_copy(source, target, load_sem.at[len(loads)])
            copy.start()
            loads.append(copy)

    def by_head(source, target):
        return [(source.at[:, pl.ds(HD * h, HD)], target.at[h]) for h in range(4)]

    def rows_of(owner, j):
        return pl.ds(pl.multiple_of(owner * 256 + HALF * j, 256), 256)

    def by_owner(owner):
        rows = [rows_of(owner, j) for j in range(2)]
        return [(source.at[r], target.at[r]) for source, target in ((x_hbm, xb), (do_hbm, dob)) for r in rows]

    load(
        (down_q_hbm, firsts.at[0]), (down_k_hbm, firsts.at[1]), (down_v_hbm, firsts.at[2]), (up_o_hbm, firsts.at[3]),
        *by_owner(1 - core), *by_owner(core), (flags_hbm, flags), *by_head(k_hbm, kb), *by_head(v_hbm, vb),
    )

    barrier = pltpu.get_barrier_semaphore()
    peers = [sibling]
    peers += [y_peer(d) for d in range(1, NY)]
    peers += [z_peer(d) for d in range(1, NZ)]
    peers += [x_peer(d) for d in range(1, NX)]
    for near in (after, before):
        peers += [{"ctx": near}, {"ctx": near, "head": y * 2 + (1 - core)}]
    for peer in peers:
        pl.semaphore_signal(barrier, inc=1, device_id=peer, device_id_type=MESH)

    sends = []

    def remote(source, target, send_sem, recv_sem, peer):
        return pltpu.make_async_remote_copy(
            src_ref=source, dst_ref=target, send_sem=send_sem, recv_sem=recv_sem,
            device_id=peer, device_id_type=MESH,
        )

    def send(*args):
        copy = remote(*args)
        copy.start()
        sends.append(copy)

    def own_latents(owner):
        first = firsts[...].reshape(4 * RANK, WIDTH)
        for j in range(2):
            rows = rows_of(owner, j)
            lat_part = dot(first[: 3 * RANK], xb[rows, :], NT)
            mix_part = dot(first[3 * RANK :], dob[rows, :], NT)
            for k in range(2):
                part[0, owner * 4 + 2 * j + k, : 3 * RANK] = lat_part[:, HD * k : HD * (k + 1)]
                part[0, owner * 4 + 2 * j + k, 3 * RANK :] = mix_part[:, HD * k : HD * (k + 1)]

    for copy in loads[:8]:
        copy.wait()
    with jax.named_scope("own_latents"):
        own_latents(1 - core)
    with jax.named_scope("entry_barrier"):
        pl.semaphore_wait(barrier, len(peers))

    mine = core * 4
    other = (1 - core) * 4

    def sum_heads(p, late=None):
        pair = (part.at[p, pl.ds(other, 4)], sib_in.at[p], sib_send.at[p], sib_recv.at[p], sibling)
        send(*pair)
        yield
        remote(*pair).wait_recv()
        extra = [0.0] * 4 if late is None else late()
        for i in range(4):
            acc[p, i] = (part[p, mine + i] + sib_in[p, i] + extra[i]).astype(BF16)
        shares = [(acc.at[p], y_in.at[p, d - 1], y_send.at[p, d - 1], y_recv.at[p, d - 1], y_peer(d)) for d in Y_ORDER]
        for share in shares:
            send(*share)
        yield
        for share in shares:
            remote(*share).wait_recv()
        for i in range(4):
            summed = acc[p, i].astype(F32)
            for d in range(1, NY):
                summed = summed + y_in[p, d - 1, i].astype(F32)
            total[p, mine + i] = summed
        own = total.at[p, pl.ds(mine, 4)]
        send(own, own, fw_send.at[p], fw_recv.at[p], sibling)
        yield
        came = total.at[p, pl.ds(other, 4)]
        remote(came, came, fw_send.at[p], fw_recv.at[p], sibling).wait_recv()
        yield

    def sum_tokens(e):
        for d in X_ORDER:
            send(cut.at[e, lax.rem(x + d, NX)], x_in.at[e, d - 1], x1_send.at[e, d - 1], x1_recv.at[e, d - 1], x_peer(d))
        yield
        summed = cut[e, x].astype(F32)
        for d in range(1, NX):
            remote(cut.at[e, 0], x_in.at[e, d - 1], x1_send.at[e, d - 1], x1_recv.at[e, d - 1], x_peer(d)).wait_recv()
            summed = summed + x_in[e, d - 1].astype(F32)
        x_sum[e] = summed.astype(BF16)
        shares = [(x_sum.at[e], z_in.at[e, d - 1], z_send.at[e, d - 1], z_recv.at[e, d - 1], z_peer(d)) for d in Z_ORDER]
        for share in shares:
            send(*share)
        yield
        summed = x_sum[e].astype(F32)
        for share in shares:
            remote(*share).wait_recv()
        for d in range(1, NZ):
            summed = summed + z_in[e, d - 1].astype(F32)
        z_all[e] = summed.astype(BF16)
        for d in X_ORDER:
            send(z_all.at[e], x_all.at[e, x], x2_send.at[e, d - 1], x2_recv.at[e, d - 1], x_peer(d))
        x_all[e, x] = z_all[e]
        yield
        for d in range(1, NX):
            came = x_all.at[e, lax.rem(x + NX - d, NX)]
            remote(z_all.at[e], came, x2_send.at[e, d - 1], x2_recv.at[e, d - 1], x_peer(d)).wait_recv()
        for c in range(4):
            out_ref[e, :, HD * c : HD * (c + 1)] = x_all[e, c].astype(F32)
        yield

    latents = sum_heads(0)
    next(latents)
    load(
        (up_q_hbm, seconds.at[0]), (up_k_hbm, seconds.at[1]), (up_v_hbm, seconds.at[2]), (down_o_hbm, seconds.at[3]),
    )
    for copy in loads[8:13]:
        copy.wait()
    with jax.named_scope("own_latents"):
        own_latents(core)

    f0, f1, f2, f3 = (flags[h] for h in range(4))
    head_of = (
        (1 - f0) * (2 - f1),
        3 * f3 + (1 - f3) * (1 + f2),
        f0 * (1 + f1),
        3 * (1 - f3) + f3 * (2 - f2),
    )
    slot_of = (
        2 - 2 * f0,
        f1 * f0 + (1 - f1) * (2 + 1 - f0),
        f2 * (f0 + f1) + (1 - f2) * (4 - f0 - f1),
        f3 + (1 - f3) * 3,
    )

    def stage_keys(slot):
        for i, base in enumerate((kb, vb)):
            kv_stage[slot, i] = base[head_of[slot], HALF:, :]
        send(kv_stage.at[slot], kv_in.at[slot], kv_send.at[slot], kv_recv.at[slot], {"ctx": after})

    for copy in loads[13:21]:
        copy.wait()
    with jax.named_scope("stage_keys"):
        stage_keys(0)
    with jax.named_scope("latent_sum"):
        next(latents)

    load(*by_head(q_hbm, qb), *by_head(dc_hbm, dcb))
    for copy in loads[21:25]:
        copy.wait()
    up_pad[...] = jnp.zeros_like(up_pad)
    for t, factor in enumerate(seconds[t] for t in range(4)):
        for copy_at in (0, RANK):
            up_pad[32 * t + copy_at : 32 * t + copy_at + RANK, WIDTH * t : WIDTH * (t + 1)] = factor
        for h in range(4):
            fac[t, h] = factor[:, HD * h : HD * (h + 1)]
    for t in range(2):
        for h in range(4):
            at = WIDTH * (1 + t) + HD * h
            prev_up[t, h] = up_pad[32:96, at : at + HD]

    with jax.named_scope("latent_sum"):
        next(latents)

    def adapt(owner):
        for j in range(2):
            rows = rows_of(owner, j)
            both = jnp.concatenate([split_rows(2.0 * total[0, owner * 4 + 2 * j + k], 4) for k in range(2)], axis=1)
            lat_low[:, rows] = both.astype(BF16)
            cols = both.T.astype(BF16)
            for t, (base, full, turned) in enumerate(
                ((kb, ka, kt), (vb, va, vt), (qb, qa, None), (dcb, ua, None))
            ):
                kind = (1, 2, 0, 3)[t]
                extra = dot(cols, up_pad[:, WIDTH * kind : WIDTH * (kind + 1)])
                for h in range(4):
                    low = (base[h, rows, :].astype(F32) + extra[:, HD * h : HD * (h + 1)]).astype(BF16)
                    full[h, rows, :] = low
                    if turned is not None:
                        turned[h, :, rows] = low.T

    for c in range(2):
        send(
            total.at[0, pl.ds(mine + 2, 2), pl.ds(RANK, 2 * RANK)], lat_prev.at[pl.ds(2 * core, 2)],
            lp_send.at[c], lp_recv.at[core], {"ctx": after, "head": y * 2 + c},
        )
    with jax.named_scope("stage_keys"):
        stage_keys(1)
    for copy in loads[25:]:
        copy.wait()
    with jax.named_scope("adapt"):
        adapt(core)
    with jax.named_scope("latent_sum"):
        next(latents)
    with jax.named_scope("adapt"):
        adapt(1 - core)

    def chunk(j, slot, at, with_off, c, sums):
        h = head_of[slot]
        off = slot if slot < 2 else None
        s, g, p, ds = (ref.at[j % 2] for ref in (score, grad_prob, prob_low, grad_low))
        ahead = HALF if with_off else 0
        length = ahead + CHUNK * (c + 1)
        strips = length // STRIP
        here = slice(at + CHUNK * c, at + CHUNK * (c + 1))
        held = {}

        def key_rows(t, b):
            first = CHUNK * b
            if first >= ahead:
                return (ka, va)[t][h, at + first - ahead : at + first - ahead + CHUNK, :]
            if off is not None:
                return off_rows[off, t, first : first + CHUNK]
            return (ka, va)[t][h, first : first + CHUNK, :]

        def key_cols(t):
            own = (kt, vt)[t][h, :, at : at + length - ahead]
            if not with_off:
                return own
            early = off_cols[off, t] if off is not None else (kt, vt)[t][h, :, :HALF]
            return jnp.concatenate([early, own], axis=1)

        def strip(i):
            return slice(STRIP * i, STRIP * (i + 1))

        def scores_of(b):
            s[CHUNK * b : CHUNK * (b + 1), :] = dot(key_rows(0, b), qa[h, here, :], NT)

        def grad_probs_of(b):
            g[CHUNK * b : CHUNK * (b + 1), :] = dot(key_rows(1, b), ua[h, here, :], NT)

        def causal(i):
            value = s[strip(i), :]
            first = STRIP * i - (length - CHUNK)
            if first < 0:
                return value
            key = lax.broadcasted_iota(jnp.int32, value.shape, 0) + first
            return jnp.where(key <= lax.broadcasted_iota(jnp.int32, value.shape, 1), value, -jnp.inf)

        def peaks(i):
            peak = fold_strip(causal(i), jnp.maximum)
            held["peak"] = peak if i == 0 else jnp.maximum(held["peak"], peak)

        def weigh(i):
            if i == 0:
                held["peak"] = jnp.max(held["peak"], axis=0, keepdims=True)
                held["sum"] = held["center"] = jnp.zeros((8, CHUNK), F32)
            weights = jnp.exp2((causal(i) - held["peak"]) * EXP_SCALE)
            s[strip(i), :] = weights
            held["sum"] = held["sum"] + fold_strip(weights, jnp.add)
            held["center"] = held["center"] + fold_strip(weights * g[strip(i), :], jnp.add)

        def finish(i):
            if i == 0:
                held["inverse"] = 1.0 / jnp.sum(held["sum"], axis=0, keepdims=True)
                held["center"] = jnp.sum(held["center"], axis=0, keepdims=True) * held["inverse"]
                held["scaled"] = held["inverse"] * SCALE
            weights = s[strip(i), :]
            p[strip(i), :] = (weights * held["inverse"]).astype(BF16)
            ds[strip(i), :] = ((weights * held["scaled"]) * (g[strip(i), :] - held["center"])).astype(BF16)

        def query_side():
            grad_q[slot, :, here] = dot(key_cols(0), ds[:length, :]).astype(BF16)

        def context_side():
            ctx_all[slot, :, here] = dot(key_cols(1), p[:length, :]).astype(BF16)

        def key_side(t, b):
            low, rows = ((ds, qa), (p, ua))[t]
            value = dot(low[CHUNK * b : CHUNK * (b + 1), :], rows[h, here, :])
            name = (t, with_off, b)
            sums[name] = sums[name] + value if name in sums else value

        blocks = range(length // CHUNK)
        before_it = [functools.partial(f, b) for b in blocks for f in (scores_of, grad_probs_of)]
        middle = [functools.partial(f, i) for f in (peaks, weigh, finish) for i in range(strips)]
        after_it = [query_side, context_side] + [functools.partial(key_side, t, b) for b in blocks for t in (0, 1)]
        return before_it, middle, after_it

    def keys_done(slot, sums):
        for t, (grad, away) in enumerate(((grad_k, back_k), (grad_v, back_v))):
            for b in range(2):
                early, late = slice(CHUNK * b, CHUNK * (b + 1)), slice(HALF + CHUNK * b, HALF + CHUNK * (b + 1))
                first, off, last = sums[t, False, b], sums[t, True, b], sums[t, True, b + 2]
                if slot < 2:
                    away[slot, early] = off.astype(BF16)
                    grad[slot, early] = last.astype(BF16)
                    grad[slot, late] = first.astype(BF16)
                else:
                    grad[slot, early] = (first + off).astype(BF16)
                    grad[slot, late] = last.astype(BF16)

    def factors(t, slots):
        return jnp.concatenate([fac[t, head_of[slot]] for slot in slots], axis=1)

    def stacked(ref, slots):
        return jnp.concatenate([ref[slot] for slot in slots], axis=0)

    def beside(ref, slots):
        return jnp.concatenate([ref[slot] for slot in slots], axis=1)

    def projections(slots):
        return [
            dot(factors(0, slots), stacked(grad_q, slots)),
            dot(factors(1, slots), beside(grad_k, slots), NT),
            dot(factors(2, slots), beside(grad_v, slots), NT),
            dot(factors(3, slots), stacked(ctx_all, slots)),
        ]

    def back_copy(c):
        return remote(
            back.at[c], back_in.at[core], back_send.at[c], back_recv.at[core],
            {"ctx": before, "head": y * 2 + c},
        )

    def latents_from_before():
        for c in range(2):
            remote(
                total.at[0, pl.ds(4 * c + 2, 2), pl.ds(RANK, 2 * RANK)], lat_prev.at[pl.ds(2 * c, 2)],
                lp_send.at[c], lp_recv.at[c], {"ctx": after},
            ).wait_recv()
        for b in range(4):
            both = split_rows(2.0 * lat_prev[b], 2)
            prev_low[:, HD * b : HD * (b + 1)] = both.astype(BF16)
            prev_cols[HD * b : HD * (b + 1), :] = both.T.astype(BF16)

    def keys_from_before(slot):
        if slot == 0:
            latents_from_before()
        remote(
            kv_stage.at[slot], kv_in.at[slot], kv_send.at[slot], kv_recv.at[slot], {"ctx": after}
        ).wait_recv()
        for t in range(2):
            extra = dot(prev_cols[...], prev_up[t, head_of[slot]])
            low = (kv_in[slot, t].astype(F32) + extra).astype(BF16)
            off_rows[slot, t] = low
            off_cols[slot, t] = low.T

    def send_back():
        for t, ref in ((1, back_k), (2, back_v)):
            value = dot(factors(t, (0, 1)), beside(ref, (0, 1)), NT)
            for b in range(4):
                back[b // 2, b % 2, RANK * (t - 1) : RANK * t] = value[:, HD * b : HD * (b + 1)]
        for c in range(2):
            back_copy(c).start()

    with jax.named_scope("attend"):
        chunks, at_start, at_end, shares = [], {}, {}, []
        all_sums = [{}, {}, {}, {}]
        order = [(0, False), (1, False), (2, False), (2, True), (0, True), (3, True), (1, True), (3, False)]
        for slot, with_off in order:
            first_at = HALF if slot < 2 else 0
            if slot < 2 and with_off:
                at_start[len(chunks)] = functools.partial(keys_from_before, slot)
            for c in ((1, 0) if (slot, with_off) == (3, False) else (0, 1)):
                at = HALF - first_at if with_off else first_at
                chunks.append(chunk(len(chunks), slot, at, with_off, c, all_sums[slot]))
            if with_off != (slot == 3):
                at_end[len(chunks) - 1] = functools.partial(keys_done, slot, all_sums[slot])
        count = len(chunks)
        for step in chunks[0][0]:
            step()
        for j in range(count + 1):
            if j + 1 in at_start:
                at_start[j + 1]()
            lists = [chunks[j][1]] if j < count else []
            lists += [chunks[j + 1][0]] if j + 1 < count else []
            lists += [chunks[j - 1][2]] if j else []
            for step in merged(*lists):
                step()
            if j - 1 in at_end:
                at_end[j - 1]()
            if j - 1 == 13:
                send_back()
            if j == count - 1:
                shares = [a + b for a, b in zip(projections((0, 1)), projections((2,)))]
        wide = jnp.concatenate([a + b for a, b in zip(shares, projections((3,)))], axis=0)

    with jax.named_scope("share_sum"):
        for b in range(8):
            part[1, place(b)] = wide[:, HD * b : HD * (b + 1)]

        def add_back():
            for c in range(2):
                remote(back.at[c], back_in.at[c], back_send.at[c], back_recv.at[c], sibling).wait_recv()
            none = jnp.zeros((RANK, HD), F32)
            return [0.0, 0.0] + [
                jnp.concatenate([none, back_in[0, i] + back_in[1, i], none], axis=0) for i in range(2)
            ]

        shares = sum_heads(1, add_back)
        next(shares)
        every = (0, 1, 2, 3)
        up_rows = [
            None,
            fold(dot(lat_low[32:64, :], beside(grad_k, every))),
            fold(dot(lat_low[64:96, :], beside(grad_v, every))),
            None,
        ]
        next(shares)
        up_rows[0] = fold(dot(lat_low[:32, :], stacked(grad_q, every), NT))
        up_rows[3] = fold(dot(lat_low[96:, :], stacked(ctx_all, every), NT))
        for t, ref in ((1, back_k), (2, back_v)):
            extra = fold(dot(prev_low[32 * t - 32 : 32 * t, :], beside(ref, (0, 1))))
            up_rows[t] = up_rows[t] + jnp.concatenate([extra, jnp.zeros_like(extra)], axis=1)
        up_rows = jnp.concatenate(up_rows, axis=0)
        for slot in every:
            up_sum[slot] = up_rows[:, HD * slot : HD * (slot + 1)]
        for h in range(4):
            cut[0, h] = up_sum[jnp.minimum(slot_of[h], 3)].astype(BF16)
        ups = sum_tokens(0)
        next(ups)
        next(shares)
        next(ups)

    def down_gradients(owner):
        wide = jnp.concatenate([split_rows(2.0 * total[1, owner * 4 + i], 4).astype(BF16) for i in range(4)], axis=1)
        down = jnp.zeros((96, WIDTH), F32)
        last = jnp.zeros((32, WIDTH), F32)
        for j in range(2):
            rows = rows_of(owner, j)
            here = wide[:, 256 * j : 256 * (j + 1)]
            down = down + dot(here[:96], xb[rows, :])
            last = last + dot(here[96:], dob[rows, :])
        return jnp.concatenate([fold(down[32 * t : 32 * t + 32]) for t in range(3)] + [fold(last)], axis=0)

    with jax.named_scope("down_gradients"):
        down = down_gradients(core)
        next(shares)
        down = down + down_gradients(1 - core)
        for c in range(4):
            cut[1, c] = down[:, HD * c : HD * (c + 1)].astype(BF16)
    with jax.named_scope("token_sum"):
        downs = sum_tokens(1)
        next(downs)
        next(downs)
        next(ups)
        next(downs)
        next(ups)
        next(downs)
    for copy in sends:
        copy.wait_send()
    for c in range(2):
        back_copy(c).wait_send()


def on_device(
    inputs, q_base, k_base, v_base, d_out, d_ctx_base, flags,
    query_down_factor, up_q, key_down_factor, up_k, value_down_factor, up_v, down_o, output_up_factor,
):
    anywhere = pl.BlockSpec(memory_space=pl.ANY)
    vmem = pl.BlockSpec(memory_space=pltpu.VMEM)
    dma = pltpu.SemaphoreType.DMA
    v = pltpu.VMEM
    out = pl.pallas_call(
        kernel,
        out_shape=pltpu.VMEM((2, 64, WIDTH), F32),
        in_specs=[anywhere] * 15,
        out_specs=vmem,
        scratch_shapes=[
            pltpu.SMEM((4,), jnp.int32), v((4, RANK, WIDTH), BF16), v((4, RANK, WIDTH), BF16),
            v((ROWS, WIDTH), BF16), *[v((4, ROWS, HD), BF16) for _ in range(3)],
            v((ROWS, WIDTH), BF16), v((4, ROWS, HD), BF16),
            v((2, 2, HALF, HD), BF16), v((2, 2, HALF, HD), BF16),
            v((2, 8, 64, HD), F32), v((2, 4, 64, HD), F32), v((2, 4, 64, HD), BF16),
            v((2, 3, 4, 64, HD), BF16), v((2, 8, 64, HD), F32),
            v((4, 32, HD), F32), v((128, 4 * WIDTH), BF16), v((4, 4, RANK, HD), BF16),
            v((2, 4, 64, HD), BF16), v((128, ROWS), BF16),
            v((64, HALF), BF16), v((HALF, 64), BF16),
            *[v((4, ROWS, HD), BF16) for _ in range(4)],
            *[v((4, HD, ROWS), BF16) for _ in range(2)],
            v((4, HD, ROWS), BF16), v((4, ROWS, HD), BF16), v((4, ROWS, HD), BF16), v((4, HD, ROWS), BF16),
            v((2, HALF, HD), BF16), v((2, HALF, HD), BF16), v((2, 2, HALF, HD), BF16), v((2, 2, HD, HALF), BF16),
            v((2, ROWS, CHUNK), F32), v((2, ROWS, CHUNK), F32), v((2, ROWS, CHUNK), BF16), v((2, ROWS, CHUNK), BF16),
            v((2, 2, 32, HD), F32), v((2, 2, 32, HD), F32), v((4, 64, HD), F32),
            v((2, 4, 64, HD), BF16), v((2, 3, 64, HD), BF16), v((2, 64, HD), BF16),
            v((2, 7, 64, HD), BF16), v((2, 64, HD), BF16), v((2, 4, 64, HD), BF16),
            dma((33,)), dma((2,)), dma((2,)), dma((2,)), dma((2,)), dma((2,)), dma((2,)),
            dma((2,)), dma((2,)), dma((2, 3)), dma((2, 3)), dma((2,)), dma((2,)),
            dma((2, 3)), dma((2, 3)), dma((2, 7)), dma((2, 7)), dma((2, 3)), dma((2, 3)),
        ],
        compiler_params=pltpu.CompilerParams(
            collective_id=0, has_side_effects=True, vmem_limit_bytes=56 * 1024 * 1024
        ),
    )(
        inputs[0], q_base[0], k_base[0], v_base[0], d_out[0], d_ctx_base[0], flags,
        query_down_factor, up_q, key_down_factor, up_k, value_down_factor, up_v, down_o, output_up_factor,
    )
    result = []
    for t in range(4):
        rows = slice(RANK * t, RANK * (t + 1))
        result += [out[1, rows], out[0, rows]]
    return (result[0], result[1], result[2], result[3], result[4], result[5], result[7], result[6])


def solution(mesh):
    tokens = P("dp", "ctx", "head")
    factor = P(None, "head")
    return jax.shard_map(
        on_device,
        mesh=mesh,
        in_specs=(tokens,) * 6 + (P("head"),) + (factor,) * 8,
        out_specs=(factor,) * 8,
        check_vma=False,
    )
```
